32 devices in a mesh: expert: 16 (over z, y, core), tensor: 2 (over x).
Axes of the slice: x: 2, y: 2, z: 4, core: 2. Of those that a mesh axis runs over, the one named last changes fastest.
Arguments:
- tokens: bfloat16 [128, 2048], P('expert', 'tensor'), may hold values from -6 to 6
- out_grad: bfloat16 [128, 2048], P('expert', 'tensor'), may hold values from -1.25 to 1.25
- expert_ids: int32 [128, 8], P('expert'), may hold values from 0 to 15, all different within a row; in each aligned block of 8 rows (0 to 7, 8 to 15, ...) at most 8 rows name the same one
- gate_probs: float32 [128, 8], P('expert'), may hold values from 0.05 to 0.45
- w_gate: bfloat16 [16, 2048, 1536], P('expert', None, 'tensor'), may hold values from -0.125 to 0.125
- w_up: bfloat16 [16, 2048, 1536], P('expert', None, 'tensor'), may hold values from -0.125 to 0.125
- w_down: bfloat16 [16, 1536, 2048], P('expert', 'tensor'), may hold values from -0.15625 to 0.15625
Outputs:
- mixed: bfloat16 [128, 2048], P('expert', 'tensor')
- token_grad: bfloat16 [128, 2048], P('expert', 'tensor')
- prob_grad: float32 [128, 8], P('expert')
The draws below stay inside these ranges and needn't reach their ends.
Inputs may be any that keep to these rules, and one draw needn't show every extreme that they name: `expert_ids`: each row names 8 different experts. Within the rows of one index of expert (aligned blocks of 8 rows) no expert is named more than 8 times, a bound that some block reaches.
All inputs are finite; a program needn't handle non-finite values.
Results may differ from the reference program's by a relative error of at most 0.02.
Values may be sent and summed in bfloat16 or wider, within the bound.
A program may use at most 64 MiB of HBM per device.

```python
import math
import jax
import jax.numpy as jnp
import numpy as np
from jax import lax

D = 2048
H = 1536
TOP = 8
TOK_GRP = 8
EXPERTS = 16
TOKENS = 128
CAP = 8
N_EXPERT = 16
N_TENSOR = 2


def block_scale(stream_key, extent, shards, smallest, high):
    def one(position, parts):
        draws = jax.random.uniform(jax.random.fold_in(jax.random.fold_in(stream_key, 6), position), (parts,), jnp.float32, smallest / len(shards), high / len(shards))
        return jnp.repeat(jnp.exp(draws), extent[position] // parts).reshape((-1,) + (1,) * (len(extent) - position - 1))

    level = one(*shards[0])
    for cut in shards[1:]:
        level = level * one(*cut)
    return level


def assign_block(key, own, number, rows, amount, top, bound, lean):
    order = jax.random.permutation(key, amount)
    crowded, usual = load_shares(amount, rows * top, bound, lean, True), load_shares(amount, rows * top, bound, lean, False)
    places = jnp.arange(amount)

    def named(tallies, turn):
        used = int((tallies > 0).sum())
        fixed = max(1, used // 4)
        passed = fixed + (places - fixed + turn * (used - fixed)) % max(1, amount - fixed)
        return jnp.zeros((amount,), jnp.int32).at[order[jnp.where(places < fixed, places, passed)]].set(jnp.asarray(tallies, jnp.int32))

    tallies = jnp.where(number % 4 == 0, named(crowded, number // 4), named(usual, number - number // 4 - 1))
    mixed = jax.random.permutation(jax.random.fold_in(own, 3), amount)
    giver, receiver = mixed[0:amount // 2 * 2:2], mixed[1:amount // 2 * 2:2]
    margin = jnp.minimum(tallies[giver] - 1, bound - tallies[receiver]) // 2
    margin = jnp.where((giver == order[0]) | (receiver == order[0]) | (tallies[receiver] == 0), 0, jnp.maximum(margin, 0))
    passed = jax.random.randint(jax.random.fold_in(own, 4), (amount // 2,), 0, 1 << 20) % (margin + 1)
    tallies = tallies.at[giver].add(-passed).at[receiver].add(passed)
    items = jnp.searchsorted(jnp.cumsum(tallies), jnp.arange(rows * top), side="right").astype(jnp.int32)
    table = items.reshape(top, rows).T
    table = table[jax.random.permutation(jax.random.fold_in(own, 1), rows)]
    turn = jax.random.randint(jax.random.fold_in(own, 2), (rows, 1), 0, top)
    return jnp.take_along_axis(table, (jnp.arange(top)[None, :] + turn) % top, axis=1)


def load_shares(number_of, total, most, skew, full):
    loads = [(1 << 20) // math.isqrt(rank ** skew) + 1 for rank in range(1, number_of + 1)]
    largest = most if full else min(most, max(-(-total // number_of), total * loads[0] // sum(loads)))
    least = 1 if total - largest >= number_of - 1 else 0
    holding, surplus = [largest] + [least] * (number_of - 1), total - largest - least * (number_of - 1)
    while surplus > 0:
        movable = [i for i in range(1, number_of) if holding[i] < largest] or [i for i in range(1, number_of) if holding[i] < most]
        whole, remaining = sum([loads[i] for i in movable]), surplus
        for i in movable:
            more = min(most - holding[i], max(1, remaining * loads[i] // whole), surplus)
            holding[i] = holding[i] + more
            surplus = surplus - more
    return np.array(holding)


def scatter_about(stream_key, extent, scale, bound, cuts=(), held_as=jnp.bfloat16):
    values = scale * jax.random.normal(stream_key, extent, jnp.float32)
    if cuts:
        values = values * block_scale(stream_key, extent, cuts, -0.22, 0.18)
    return jnp.clip(values, -bound, bound).astype(held_as)


def setup_inputs(seed: int = 0) -> dict:
    key_list = jax.random.split(jax.random.key(seed), 8)
    tokens = scatter_about(key_list[0], (TOKENS, D), 1.0, 6.0, ((0, 16), (1, 2)))
    out_grad = scatter_about(key_list[1], (TOKENS, D), 0.2, 1.25, ((0, 16), (1, 2)))
    expert_ids_keys = jax.random.split(jax.random.fold_in(key_list[2], 1), TOKENS // TOK_GRP)
    expert_ids_turns = jax.random.permutation(jax.random.fold_in(key_list[2], 3), TOKENS // TOK_GRP)
    expert_ids = jax.vmap(lambda own, number: assign_block(jax.random.fold_in(key_list[2], 2), own, number, TOK_GRP, EXPERTS, TOP, CAP, 2))(expert_ids_keys, expert_ids_turns).reshape((TOKENS, TOP))
    gate_probs = jnp.clip(0.05 + 0.39999999 * jax.random.uniform(key_list[3], (TOKENS, TOP), jnp.float32) ** block_scale(key_list[3], (TOKENS, TOP), ((0, 16),), -0.2, 0.2), 0.05, 0.45)
    w_gate = scatter_about(key_list[4], (EXPERTS, D, H), D ** -0.5, 0.125, ((0, 16), (2, 2)))
    w_up = scatter_about(key_list[5], (EXPERTS, D, H), D ** -0.5, 0.125, ((0, 16), (2, 2)))
    w_down = scatter_about(key_list[6], (EXPERTS, H, D), H ** -0.5, 0.15625, ((0, 16), (1, 2)))
    return dict(tokens=tokens, out_grad=out_grad, expert_ids=expert_ids, gate_probs=gate_probs, w_gate=w_gate, w_up=w_up, w_down=w_down)


def slot_index(group_ids, expert_count, capacity):
    flat_ids = group_ids.reshape(-1).astype(jnp.int32)
    onehot = (flat_ids[:, None] == jnp.arange(expert_count, dtype=jnp.int32)[None, :]).astype(jnp.int32)
    before = jnp.cumsum(onehot, axis=0) - onehot
    slot_rank = jnp.sum(before * onehot, axis=1)
    return (flat_ids * capacity + slot_rank).astype(jnp.int32)


def expert_pass(operands):
    slot_tokens, slot_grads, gate_w, up_w, down_w = operands
    row_count = slot_tokens.shape[0]
    block_width = H // N_TENSOR
    gate_pre = jnp.dot(slot_tokens, gate_w, preferred_element_type=jnp.float32)
    up_pre = jnp.dot(slot_tokens, up_w, preferred_element_type=jnp.float32)
    gate_sig = jax.nn.sigmoid(gate_pre)
    hidden = (gate_pre * gate_sig * up_pre).astype(jnp.bfloat16)
    partials = jnp.einsum("rth,thd->trd", hidden.reshape(row_count, N_TENSOR, block_width).astype(jnp.float32),
                          down_w.reshape(N_TENSOR, block_width, D).astype(jnp.float32),
                          precision=lax.Precision.HIGHEST)
    partials = lax.optimization_barrier(partials.astype(jnp.bfloat16))
    expert_out = jnp.sum(partials.astype(jnp.float32), axis=0).astype(jnp.bfloat16)
    hidden_grad = jnp.dot(slot_grads, down_w.T, preferred_element_type=jnp.float32)
    grad_gate = (hidden_grad * up_pre * gate_sig * (1.0 + gate_pre * (1.0 - gate_sig))).astype(jnp.bfloat16)
    grad_up = (hidden_grad * gate_pre * gate_sig).astype(jnp.bfloat16)
    back_parts = jnp.einsum("rth,dth->trd", grad_gate.reshape(row_count, N_TENSOR, block_width).astype(jnp.float32),
                            gate_w.reshape(D, N_TENSOR, block_width).astype(jnp.float32),
                            precision=lax.Precision.HIGHEST)
    back_parts = back_parts + jnp.einsum("rth,dth->trd", grad_up.reshape(row_count, N_TENSOR, block_width).astype(jnp.float32),
                                         up_w.reshape(D, N_TENSOR, block_width).astype(jnp.float32),
                                         precision=lax.Precision.HIGHEST)
    back_parts = lax.optimization_barrier(back_parts.astype(jnp.bfloat16))
    expert_back = jnp.sum(back_parts.astype(jnp.float32), axis=0).astype(jnp.bfloat16)
    return expert_out, expert_back


def reference(tokens, out_grad, expert_ids, gate_probs, w_gate, w_up, w_down):
    group_count = N_EXPERT
    slot_total = EXPERTS * CAP
    slot_ids = jax.vmap(lambda group_ids: slot_index(group_ids, EXPERTS, CAP))(expert_ids.reshape(group_count, TOK_GRP, TOP))
    token_groups = tokens.reshape(group_count, TOK_GRP, D)
    grad_groups = out_grad.reshape(group_count, TOK_GRP, D)
    prob_groups = gate_probs.reshape(group_count, TOK_GRP, TOP)
    token_copies = jnp.repeat(token_groups, TOP, axis=1)
    grad_copies = (prob_groups.reshape(group_count, TOK_GRP * TOP)[:, :, None]
                   * jnp.repeat(grad_groups, TOP, axis=1).astype(jnp.float32)).astype(jnp.bfloat16)

    def place(slot_row, values):
        return jnp.zeros((slot_total, D), values.dtype).at[slot_row].set(values)

    token_slots = jax.vmap(place)(slot_ids, token_copies)
    grad_slots = jax.vmap(place)(slot_ids, grad_copies)

    def to_experts(slot_array):
        return slot_array.reshape(group_count, EXPERTS, CAP, D).transpose(1, 0, 2, 3).reshape(EXPERTS, group_count * CAP, D)

    def to_groups(expert_array):
        return expert_array.reshape(EXPERTS, group_count, CAP, D).transpose(1, 0, 2, 3).reshape(group_count, slot_total, D)

    expert_out, expert_back = lax.map(expert_pass, (to_experts(token_slots), to_experts(grad_slots), w_gate, w_up, w_down))
    out_groups = to_groups(expert_out)
    back_groups = to_groups(expert_back)
    token_out = jax.vmap(lambda table, slot_row: table[slot_row])(out_groups, slot_ids).reshape(group_count, TOK_GRP, TOP, D)
    token_back = jax.vmap(lambda table, slot_row: table[slot_row])(back_groups, slot_ids).reshape(group_count, TOK_GRP, TOP, D)
    mixed = jnp.einsum("ngk,ngkd->ngd", prob_groups, token_out.astype(jnp.float32),
                       precision=lax.Precision.HIGHEST).astype(jnp.bfloat16)
    prob_grad = jnp.einsum("ngd,ngkd->ngk", grad_groups.astype(jnp.float32), token_out.astype(jnp.float32),
                           precision=lax.Precision.HIGHEST)
    token_grad = jnp.sum(token_back.astype(jnp.float32), axis=2).astype(jnp.bfloat16)
    return (mixed.reshape(TOKENS, D), token_grad.reshape(TOKENS, D), prob_grad.reshape(TOKENS, TOP))
```

```python
import functools

import jax
import jax.numpy as jnp
from jax import lax
from jax.experimental import pallas as pl
from jax.experimental.pallas import tpu as pltpu
from jax.sharding import PartitionSpec as P

CORES = 2
LANES = 128
MESH = pl.DeviceIdType.MESH


def grid_of(expert_count):
    chips = expert_count // CORES
    fast = 1
    while (fast * 2) * (fast * 2) <= chips:
        fast *= 2
    return chips // fast, fast


def dot_nn(left, right):
    return jnp.dot(left, right, preferred_element_type=jnp.float32)


def dot_nt(left, right):
    return lax.dot_general(
        left, right, (((1,), (1,)), ((), ())), preferred_element_type=jnp.float32
    )


def kernel(
    A, B, T, count,
    tok_ref, grad_ref, ids_ref, prob_ref, wg_hbm, wu_hbm, wd_hbm,
    mixed_ref, tgrad_ref, pgrad_ref,
    wg, wu, wd, g0, g1, pg, xs, og, hid, gga, gup,
    r0, r1, rc0, rc1, s0, s1, rx0, ry1, u0, u1, ry0, rx1, v0, v1, rz0, rz1,
    qr, qc, qx, qt, qy, qv, qz,
    wsem, ssem, rsem,
):
    me = lax.axis_index("expert")
    t = lax.axis_index("tensor")
    c = lax.rem(me, CORES)
    b = lax.rem(lax.div(me, CORES), B)
    a = lax.div(me, CORES * B)
    group, feats = tok_ref.shape
    half = feats // 2
    lanes = pg.shape[-1]
    rows = xs.shape[0]

    def spot(aa, bb, cc, tt):
        return ((aa * B + bb) * CORES + cc, tt)

    def turn(value, r, size):
        return lax.rem(value + r, size)

    to_a = [spot(turn(a, r, A), b, c, t) for r in range(1, A)]
    to_b = [spot(a, turn(b, r, B), c, t) for r in range(1, B)]
    to_t = [spot(a, b, c, turn(t, r, T)) for r in range(1, T)]
    to_c = spot(a, b, 1 - c, t)

    loads = [
        pltpu.make_async_copy(src.at[0], dst, wsem.at[i])
        for i, (src, dst) in enumerate(((wg_hbm, wg), (wu_hbm, wu), (wd_hbm, wd)))
    ]
    for load in loads:
        load.start()

    barrier = pltpu.get_barrier_semaphore()
    peers = to_a + to_b + to_t + [to_c]
    for peer in peers:
        pl.semaphore_signal(barrier, inc=1, device_id=peer, device_id_type=MESH)

    ids = ids_ref[...]
    probs = prob_ref[...]
    lane = lax.broadcasted_iota(jnp.int32, (group, lanes), 1)
    routed = jnp.zeros((group, lanes), jnp.float32)
    for k in range(ids.shape[1]):
        routed = routed + jnp.where(lane == ids[:, k : k + 1], probs[:, k : k + 1], 0.0)
    unit = jnp.concatenate(
        [tok_ref[...].astype(jnp.float32), grad_ref[...].astype(jnp.float32)], axis=0
    ).astype(jnp.bfloat16)
    g0[c, t, b, a] = unit[:, :half]
    g1[c, b, t, a] = unit[:, half:]
    pg[c, b, a] = routed
    pl.semaphore_wait(barrier, len(peers))

    started = []

    def send(src, dst, peer):
        i = len(started)
        copy = pltpu.make_async_remote_copy(
            src_ref=src, dst_ref=dst, send_sem=ssem.at[i], recv_sem=rsem.at[i],
            device_id=peer, device_id_type=MESH,
        )
        copy.start()
        started.append(copy)
        return copy

    def same(ref, peers):
        return [send(ref, ref, peer) for peer in peers]

    def arrive(copies):
        for copy in copies:
            copy.wait_recv()

    a0 = same(g0.at[c, t, b, a], to_a)
    a1 = same(g1.at[c, b, t, a], to_a)
    ap = same(pg.at[c, b, a], to_a)
    arrive(a0)
    b0 = same(g0.at[c, t, b], to_b)
    arrive(a1)
    b1 = same(g1.at[c, b, t], to_t)
    arrive(ap)
    bp = same(pg.at[c, b], to_b)
    arrive(b0)
    c0 = same(g0.at[c, t], to_t)
    arrive(b1)
    c1 = same(g1.at[c, b], to_b)
    arrive(bp)
    dp = same(pg.at[c], [to_c])
    arrive(c0)
    d0 = same(g0.at[c], [to_c])
    arrive(c1)
    d1 = same(g1.at[c], [to_c])
    arrive(dp)
    arrive(d0)
    arrive(d1)

    part = B * A * group
    for cc in range(CORES):
        for tt in range(T):
            for h in range(2):
                block = g0[cc, tt] if h == 0 else g1[cc, :, tt]
                block = block.astype(jnp.float32)
                at = (pl.ds(cc * part, part), pl.ds(tt * feats + h * half, half))
                xs[at] = block[:, :, :group].reshape(part, half).astype(jnp.bfloat16)
                og[at] = block[:, :, group:].reshape(part, half).astype(jnp.bfloat16)

    for load in loads:
        load.wait()

    step = min(rows, 256)
    tiles = step // group

    def first(i):
        at = pl.ds(i * step if isinstance(i, int) else pl.multiple_of(i * step, step), step)
        weights = pg.reshape(rows, lanes)[at, :]
        mine = lax.broadcasted_iota(jnp.int32, (step, lanes), 1) == me
        weight = jnp.sum(jnp.where(mine, weights, 0.0), axis=1, keepdims=True)
        gate = dot_nn(xs[at, :], wg[...])
        up = dot_nn(xs[at, :], wu[...])
        back = dot_nt(og[at, :], wd[...])
        sig = jax.nn.sigmoid(gate)
        silu = gate * sig
        hidden = silu * up
        inner = jnp.sum(hidden * back, axis=1, keepdims=True)
        back = back * weight
        hid[at, :] = (hidden * weight).astype(jnp.bfloat16)
        gga[at, :] = (back * up * sig * (1.0 + gate * (1.0 - sig))).astype(jnp.bfloat16)
        gup[at, :] = (back * silu).astype(jnp.bfloat16)
        qr.reshape(rows, lanes)[at, :] = jnp.where(mine, inner, 0.0)

    if rows == step:
        first(0)
    else:
        pl.loop(0, rows // step)(first)

    ec = send(qr.at[1 - c], qc, to_c)

    cuts = CORES if rows > 256 else 1

    def second(h, r):
        tt = turn(t, r, T)
        ref, landing = ((r0, rc0), (r1, rc1))[h]
        cols = pl.ds(pl.multiple_of(tt * feats + h * half, half), half)
        size = rows // cuts
        for i in range(cuts):
            at = pl.ds(i * size, size)
            out = dot_nn(hid[at, :], wd[:, cols])
            back = dot_nt(gga[at, :], wg[cols, :]) + dot_nt(gup[at, :], wu[cols, :])
            shape = (CORES // cuts, B, A, group, half)
            block = jnp.concatenate([out.reshape(shape), back.reshape(shape)], axis=3)
            block = block.astype(jnp.bfloat16)
            for j in range(CORES // cuts):
                ref[i + j, tt] = block[j]
        return send(ref.at[1 - c, tt], landing.at[tt], to_c)

    def wide(value):
        return value.astype(jnp.float32)

    def narrow(value):
        return value.astype(jnp.bfloat16)

    def total(first_term, ref):
        value = wide(first_term)
        for i in range(ref.shape[0]):
            value = value + wide(ref[i])
        return value

    e0 = [second(0, r) for r in list(range(1, T)) + [0]]
    f0 = []
    for r in range(1, T):
        e0[r - 1].wait_recv()
        tt = turn(t, r, T)
        s0[tt] = narrow(wide(r0[c, tt]) + wide(rc0[tt]))
        f0.append(send(s0.at[tt], rx0.at[r - 1], to_t[r - 1]))
    e1 = [second(1, r) for r in list(range(1, T)) + [0]]
    ec.wait_recv()
    qx[t] = qr[c] + qc[...]
    fq = same(qx.at[t], to_t)
    e0[T - 1].wait_recv()
    s0[t] = narrow(wide(r0[c, t]) + wide(rc0[t]))
    arrive(e1)
    f1 = []
    for r in list(range(1, B)) + [0]:
        bb = turn(b, r, B)
        s1[bb] = narrow(wide(r1[c, :, bb]) + wide(rc1[:, bb]))
        if r:
            f1.append(send(s1.at[bb], ry1.at[r - 1], to_b[r - 1]))
    arrive(f0)
    u0[...] = narrow(total(s0[t], rx0))
    h0 = [send(u0.at[turn(b, r, B)], ry0.at[r - 1], to_b[r - 1]) for r in range(1, B)]
    arrive(fq)
    value = qx[0]
    for i in range(1, T):
        value = value + qx[i]
    qt[...] = value
    hq = [send(qt.at[turn(b, r, B)], qy.at[r - 1], to_b[r - 1]) for r in range(1, B)]
    arrive(f1)
    u1[...] = narrow(total(s1[b], ry1))
    h1 = [send(u1.at[turn(t, r, T)], rx1.at[r - 1], to_t[r - 1]) for r in range(1, T)]
    arrive(h0)
    v0[...] = narrow(total(u0[b], ry0))
    k0 = [send(v0.at[turn(a, r, A)], rz0.at[r - 1], to_a[r - 1]) for r in range(1, A)]
    arrive(hq)
    qv[...] = total(qt[b], qy)
    kq = [send(qv.at[turn(a, r, A)], qz.at[r - 1], to_a[r - 1]) for r in range(1, A)]
    arrive(h1)
    v1[...] = narrow(total(u1[t], rx1))
    k1 = [send(v1.at[turn(a, r, A)], rz1.at[r - 1], to_a[r - 1]) for r in range(1, A)]
    arrive(k0)
    last = total(v0[a], rz0)
    mixed_ref[:, :half] = narrow(last[:group])
    tgrad_ref[:, :half] = narrow(last[group:])
    arrive(kq)
    inner = total(qv[a], qz)
    column = lax.broadcasted_iota(jnp.int32, ids.shape, 1)
    result = jnp.zeros(ids.shape, jnp.float32)
    for k in range(ids.shape[1]):
        one = jnp.sum(jnp.where(lane == ids[:, k : k + 1], inner, 0.0), axis=1, keepdims=True)
        result = jnp.where(column == k, one, result)
    pgrad_ref[...] = result
    arrive(k1)
    last = total(v1[a], rz1)
    mixed_ref[:, half:] = narrow(last[:group])
    tgrad_ref[:, half:] = narrow(last[group:])
    assert len(started) == count
    for copy in started:
        copy.wait_send()


def per_device(tokens, out_grad, expert_ids, gate_probs, w_gate, w_up, w_down):
    E = lax.axis_size("expert")
    T = lax.axis_size("tensor")
    A, B = grid_of(E)
    C = CORES
    group, feats = tokens.shape
    width = feats * T
    hidden = w_gate.shape[2]
    half = feats // 2
    rows = E * group
    lanes = -(-E // LANES) * LANES
    bf, f32 = jnp.bfloat16, jnp.float32
    pair = (2 * group, half)
    tile = (group, lanes)
    na, nb, nt = A - 1, B - 1, T - 1
    count = 3 * na + 2 * nb + nt + nt + nb + 3 + 1 + 2 * T + 2 * nt + nb + 2 * nb + nt + 3 * na

    def vm(*shape, dtype=bf):
        return pltpu.VMEM(shape, dtype)

    scratch = [
        vm(width, hidden), vm(width, hidden), vm(hidden, width),
        vm(C, T, B, A, *pair), vm(C, B, T, A, *pair), vm(C, B, A, *tile, dtype=f32),
        vm(rows, width), vm(rows, width),
        vm(rows, hidden), vm(rows, hidden), vm(rows, hidden),
        vm(C, T, B, A, *pair), vm(C, T, B, A, *pair),
        vm(T, B, A, *pair), vm(T, B, A, *pair),
        vm(T, B, A, *pair), vm(B, T, A, *pair),
        vm(nt, B, A, *pair), vm(nb, T, A, *pair),
        vm(B, A, *pair), vm(T, A, *pair),
        vm(nb, A, *pair), vm(nt, A, *pair),
        vm(A, *pair), vm(A, *pair),
        vm(na, *pair), vm(na, *pair),
        vm(C, B, A, *tile, dtype=f32), vm(B, A, *tile, dtype=f32),
        vm(T, B, A, *tile, dtype=f32), vm(B, A, *tile, dtype=f32),
        vm(nb, A, *tile, dtype=f32), vm(A, *tile, dtype=f32),
        vm(na, *tile, dtype=f32),
        pltpu.SemaphoreType.DMA((3,)),
        pltpu.SemaphoreType.DMA((count,)),
        pltpu.SemaphoreType.DMA((count,)),
    ]
    inside = pl.BlockSpec(memory_space=pltpu.VMEM)
    outside = pl.BlockSpec(memory_space=pl.ANY)
    return pl.pallas_call(
        functools.partial(kernel, A, B, T, count),
        out_shape=(
            jax.ShapeDtypeStruct((group, feats), bf),
            jax.ShapeDtypeStruct((group, feats), bf),
            jax.ShapeDtypeStruct(expert_ids.shape, f32),
        ),
        in_specs=[inside] * 4 + [outside] * 3,
        out_specs=(inside, inside, inside),
        scratch_shapes=scratch,
        compiler_params=pltpu.CompilerParams(
            collective_id=0, has_side_effects=True, vmem_limit_bytes=58 * 1024 * 1024
        ),
        cost_estimate=pl.CostEstimate(
            flops=12 * rows * width * hidden,
            bytes_accessed=6 * width * hidden,
            transcendentals=rows * hidden,
        ),
    )(tokens, out_grad, expert_ids, gate_probs, w_gate, w_up, w_down)


def solution(mesh):
    placed = (
        P("expert", "tensor"),
        P("expert", "tensor"),
        P("expert", None),
        P("expert", None),
        P("expert", None, "tensor"),
        P("expert", None, "tensor"),
        P("expert", "tensor", None),
    )
    return jax.shard_map(
        per_device,
        mesh=mesh,
        in_specs=placed,
        out_specs=(P("expert", "tensor"), P("expert", "tensor"), P("expert", None)),
        check_vma=False,
    )
```

```python
import functools

import jax
import jax.numpy as jnp
from jax import lax
from jax.experimental import pallas as pl
from jax.experimental.pallas import tpu as pltpu
from jax.sharding import PartitionSpec as P

CORES = 2
LANES = 128
PATHS = 2
PIECES = 2
MESH = pl.DeviceIdType.MESH


def grid_of(expert_count):
    chips = expert_count // CORES
    fast = 1
    while (fast * 2) * (fast * 2) <= chips:
        fast *= 2
    return chips // fast, fast


def dot_nn(left, right):
    return jnp.dot(left, right, preferred_element_type=jnp.float32)


def dot_nt(left, right):
    return lax.dot_general(
        left, right, (((1,), (1,)), ((), ())), preferred_element_type=jnp.float32
    )


def kernel(
    A, B, T, count,
    tok_ref, grad_ref, ids_ref, prob_ref, wg_hbm, wu_hbm, wd_hbm,
    mixed_ref, tgrad_ref, pgrad_ref,
    wg, wu, wd, g0, g1, pg, xs, og, hid, gga, gup, sum_gate, sum_up, sum_back,
    r0, r1, rc0, rc1, s0, s1, rx0, ry1, u0, u1, ry0, rx1, v0, v1, rz0, rz1,
    qr, qc, qx, qt, qy, qv, qz,
    wsem, ssem, rsem,
):
    me = lax.axis_index("expert")
    t = lax.axis_index("tensor")
    c = lax.rem(me, CORES)
    b = lax.rem(lax.div(me, CORES), B)
    a = lax.div(me, CORES * B)
    group, feats = tok_ref.shape
    piece = feats // (PATHS * PIECES)
    lanes = pg.shape[-1]
    rows = xs.shape[0]
    pieces = range(PIECES)

    def spot(aa, bb, cc, tt):
        return ((aa * B + bb) * CORES + cc, tt)

    def turn(value, r, size):
        return lax.rem(value + r, size)

    def column(h, s):
        return (s * PATHS + h) * piece

    to_a = [spot(turn(a, r, A), b, c, t) for r in range(1, A)]
    to_b = [spot(a, turn(b, r, B), c, t) for r in range(1, B)]
    to_t = [spot(a, b, c, turn(t, r, T)) for r in range(1, T)]
    to_c = spot(a, b, 1 - c, t)

    loads = [
        pltpu.make_async_copy(src.at[0], dst, wsem.at[i])
        for i, (src, dst) in enumerate(((wg_hbm, wg), (wu_hbm, wu), (wd_hbm, wd)))
    ]

    barrier = pltpu.get_barrier_semaphore()
    peers = to_a + to_b + to_t + [to_c]
    for peer in peers:
        pl.semaphore_signal(barrier, inc=1, device_id=peer, device_id_type=MESH)
    for load in loads:
        load.start()

    ids = ids_ref[...]
    probs = prob_ref[...]
    lane = lax.broadcasted_iota(jnp.int32, (group, lanes), 1)
    routed = jnp.zeros((group, lanes), jnp.float32)
    for k in range(ids.shape[1]):
        routed = routed + jnp.where(lane == ids[:, k : k + 1], probs[:, k : k + 1], 0.0)
    unit = jnp.concatenate(
        [tok_ref[...].astype(jnp.float32), grad_ref[...].astype(jnp.float32)], axis=0
    ).astype(jnp.bfloat16)
    for s in pieces:
        g0[s, c, t, b, a] = unit[:, column(0, s) : column(0, s) + piece]
        g1[s, c, b, t, a] = unit[:, column(1, s) : column(1, s) + piece]
    pg[c, b, a] = routed
    pl.semaphore_wait(barrier, len(peers))

    started = []

    def send(src, dst, peer):
        i = len(started)
        copy = pltpu.make_async_remote_copy(
            src_ref=src, dst_ref=dst, send_sem=ssem.at[i], recv_sem=rsem.at[i],
            device_id=peer, device_id_type=MESH,
        )
        copy.start()
        started.append(copy)
        return copy

    def same(ref, peers):
        return [send(ref, ref, peer) for peer in peers]

    def arrive(copies):
        for copy in copies:
            copy.wait_recv()

    a0, a1, b0, b1, c0, c1 = ([None] * PIECES for _ in range(6))
    for s in pieces:
        a0[s] = same(g0.at[s, c, t, b, a], to_a)
        a1[s] = same(g1.at[s, c, b, t, a], to_a)
    ap = same(pg.at[c, b, a], to_a)
    for s in pieces:
        arrive(a0[s])
        b0[s] = same(g0.at[s, c, t, b], to_b)
        arrive(a1[s])
        b1[s] = same(g1.at[s, c, b, t], to_t)
    arrive(ap)
    bp = same(pg.at[c, b], to_b)
    own, rest0, rest1 = [], [], []
    for s in pieces:
        arrive(b0[s])
        c0[s] = same(g0.at[s, c, t], to_t)
        own += same(g0.at[s, c, t], [to_c])
        arrive(b1[s])
        c1[s] = same(g1.at[s, c, b], to_b)
        rest1.append(same(g1.at[s, c, b], [to_c]))
    arrive(bp)
    dp = same(pg.at[c], [to_c])

    part = B * A * group
    step = min(rows, 256)

    def assemble(slot, h, s, r):
        tt = turn(t, r, T)
        for cc in range(CORES):
            block = g0[s, cc, tt] if h == 0 else g1[s, cc, :, tt]
            block = block.astype(jnp.float32)
            at = (pl.ds(cc * part, part), pl.ds(slot * piece, piece))
            xs[at] = block[:, :, :group].reshape(part, piece).astype(jnp.bfloat16)
            og[at] = block[:, :, group:].reshape(part, piece).astype(jnp.bfloat16)

    def products(at, runs):
        gate = up = back = None
        for slot, h, s, r, width in runs:
            start = pl.multiple_of(turn(t, r, T) * feats + column(h, s), piece)
            here = pl.ds(slot * piece, width * piece)
            there = pl.ds(start, width * piece)
            x, o = xs[at, here], og[at, here]
            terms = dot_nn(x, wg[there, :]), dot_nn(x, wu[there, :]), dot_nt(o, wd[:, there])
            if gate is None:
                gate, up, back = terms
            else:
                gate, up, back = gate + terms[0], up + terms[1], back + terms[2]
        return gate, up, back

    def by_rows(body):
        if rows == step:
            body(pl.ds(0, rows))
        else:

            @pl.loop(0, rows // step)
            def _(i):
                body(pl.ds(pl.multiple_of(i * step, step), step))

    slots = 0

    def plan(runs):
        nonlocal slots
        out = []
        for h, s, r, width in runs:
            for i in range(width):
                assemble(slots + i, h + i, s, r)
            out.append((slots, h, s, r, width))
            slots += width
        return out

    def forward0(s):
        for r in range(1, T):
            c0[s][r - 1].wait_recv()
            rest0.append(same(g0.at[s, c, turn(t, T - r, T)], [to_c]))

    def forward1(s):
        for r in range(1, B):
            c1[s][r - 1].wait_recv()
            rest1.append(same(g1.at[s, c, turn(b, B - r, B)], [to_c]))

    forward0(0)
    for load in loads:
        load.wait()
    arrive(own)
    runs = plan([(0, s, 0, 1) for s in pieces])

    def begin(at):
        sum_gate[at, :], sum_up[at, :], sum_back[at, :] = products(at, runs)

    by_rows(begin)
    for s in pieces:
        forward1(s)
        if s:
            forward0(s)
    for copies in rest0 + rest1:
        arrive(copies)
    arrive(dp)
    more = plan(
        [(0, s, r, 2) for s in pieces for r in range(1, T)] + [(1, s, 0, 1) for s in pieces]
    )

    def finish(at):
        gate, up, back = products(at, more)
        gate = gate + sum_gate[at, :]
        up = up + sum_up[at, :]
        back = back + sum_back[at, :]
        weights = pg.reshape(rows, lanes)[at, :]
        mine = lax.broadcasted_iota(jnp.int32, (step, lanes), 1) == me
        weight = jnp.sum(jnp.where(mine, weights, 0.0), axis=1, keepdims=True)
        sig = jax.nn.sigmoid(gate)
        silu = gate * sig
        hidden = silu * up
        inner = jnp.sum(hidden * back, axis=1, keepdims=True)
        back = back * weight
        hid[at, :] = (hidden * weight).astype(jnp.bfloat16)
        gga[at, :] = (back * up * sig * (1.0 + gate * (1.0 - sig))).astype(jnp.bfloat16)
        gup[at, :] = (back * silu).astype(jnp.bfloat16)
        qr.reshape(rows, lanes)[at, :] = jnp.where(mine, inner, 0.0)

    by_rows(finish)
    ec = send(qr.at[1 - c], qc, to_c)

    cuts = CORES if rows > 256 else 1

    def second(h, s, r):
        tt = turn(t, r, T)
        ref, landing = ((r0, rc0), (r1, rc1))[h]
        cols = pl.ds(pl.multiple_of(tt * feats + column(h, s), piece), piece)
        size = rows // cuts
        for i in range(cuts):
            at = pl.ds(i * size, size)
            out = dot_nn(hid[at, :], wd[:, cols])
            back = dot_nt(gga[at, :], wg[cols, :]) + dot_nt(gup[at, :], wu[cols, :])
            shape = (CORES // cuts, B, A, group, piece)
            block = jnp.concatenate([out.reshape(shape), back.reshape(shape)], axis=3)
            block = block.astype(jnp.bfloat16)
            for j in range(CORES // cuts):
                ref[s, i + j, tt] = block[j]
        return send(ref.at[s, 1 - c, tt], landing.at[s, tt], to_c)

    def wide(value):
        return value.astype(jnp.float32)

    def narrow(value):
        return value.astype(jnp.bfloat16)

    def total(first_term, ref):
        value = wide(first_term)
        for i in range(ref.shape[0]):
            value = value + wide(ref[i])
        return value

    far = list(range(1, T))
    e0 = [[None] * T for _ in pieces]
    e1 = [[None] * T for _ in pieces]
    f0, f1, h0, h1, k0, k1 = ([None] * PIECES for _ in range(6))

    def away0(s):
        f0[s] = []
        for r in far:
            e0[s][r].wait_recv()
            tt = turn(t, r, T)
            s0[s, tt] = narrow(wide(r0[s, c, tt]) + wide(rc0[s, tt]))
            f0[s].append(send(s0.at[s, tt], rx0.at[s, r - 1], to_t[r - 1]))

    def home0(s):
        e0[s][0].wait_recv()
        s0[s, t] = narrow(wide(r0[s, c, t]) + wide(rc0[s, t]))

    def away1(s):
        arrive(e1[s])
        f1[s] = []
        for r in list(range(1, B)) + [0]:
            bb = turn(b, r, B)
            s1[s, bb] = narrow(wide(r1[s, c, :, bb]) + wide(rc1[s, :, bb]))
            if r:
                f1[s].append(send(s1.at[s, bb], ry1.at[s, r - 1], to_b[r - 1]))

    def across0(s):
        arrive(f0[s])
        u0[s] = narrow(total(s0[s, t], rx0.at[s]))
        h0[s] = [
            send(u0.at[s, turn(b, r, B)], ry0.at[s, r - 1], to_b[r - 1]) for r in range(1, B)
        ]

    def across1(s):
        arrive(f1[s])
        u1[s] = narrow(total(s1[s, b], ry1.at[s]))
        h1[s] = [
            send(u1.at[s, turn(t, r, T)], rx1.at[s, r - 1], to_t[r - 1]) for r in range(1, T)
        ]

    def along0(s):
        arrive(h0[s])
        v0[s] = narrow(total(u0[s, b], ry0.at[s]))
        k0[s] = [
            send(v0.at[s, turn(a, r, A)], rz0.at[s, r - 1], to_a[r - 1]) for r in range(1, A)
        ]

    def along1(s):
        arrive(h1[s])
        v1[s] = narrow(total(u1[s, t], rx1.at[s]))
        k1[s] = [
            send(v1.at[s, turn(a, r, A)], rz1.at[s, r - 1], to_a[r - 1]) for r in range(1, A)
        ]

    for s in pieces:
        for r in far:
            e0[s][r] = second(0, s, r)
        if s:
            home0(s - 1)
        for r in far:
            e1[s][r] = second(1, s, r)
        away0(s)
        if s:
            across0(s - 1)
        else:
            ec.wait_recv()
            qx[t] = qr[c] + qc[...]
            fq = same(qx.at[t], to_t)
        e1[s][0] = second(1, s, 0)
        e0[s][0] = second(0, s, 0)
        away1(s)
    last = PIECES - 1
    for s in range(last):
        across1(s)
    home0(last)
    arrive(fq)
    value = qx[0]
    for i in range(1, T):
        value = value + qx[i]
    qt[...] = value
    hq = [send(qt.at[turn(b, r, B)], qy.at[r - 1], to_b[r - 1]) for r in range(1, B)]
    for s in range(last):
        along0(s)
    across0(last)
    arrive(hq)
    qv[...] = total(qt[b], qy)
    kq = [send(qv.at[turn(a, r, A)], qz.at[r - 1], to_a[r - 1]) for r in range(1, A)]
    for s in range(last):
        along1(s)
    across1(last)
    along0(last)

    def deliver(h, s, mine, ref, copies):
        arrive(copies)
        value = total(mine, ref)
        at = pl.ds(column(h, s), piece)
        mixed_ref[:, at] = narrow(value[:group])
        tgrad_ref[:, at] = narrow(value[group:])

    for s in range(last):
        deliver(0, s, v0[s, a], rz0.at[s], k0[s])
    arrive(kq)
    inner = total(qv[a], qz)
    place = lax.broadcasted_iota(jnp.int32, ids.shape, 1)
    result = jnp.zeros(ids.shape, jnp.float32)
    for k in range(ids.shape[1]):
        one = jnp.sum(jnp.where(lane == ids[:, k : k + 1], inner, 0.0), axis=1, keepdims=True)
        result = jnp.where(place == k, one, result)
    pgrad_ref[...] = result
    along1(last)
    for s in range(last):
        deliver(1, s, v1[s, a], rz1.at[s], k1[s])
    deliver(0, last, v0[last, a], rz0.at[last], k0[last])
    deliver(1, last, v1[last, a], rz1.at[last], k1[last])
    assert len(started) == count
    for copy in started:
        copy.wait_send()


def settle(*refs):
    for source, target in zip(refs[: len(refs) // 2], refs[len(refs) // 2 :]):
        target[...] = source[...]


def per_device(tokens, out_grad, expert_ids, gate_probs, w_gate, w_up, w_down):
    E = lax.axis_size("expert")
    T = lax.axis_size("tensor")
    A, B = grid_of(E)
    C, S = CORES, PIECES
    group, feats = tokens.shape
    width = feats * T
    hidden = w_gate.shape[2]
    rows = E * group
    lanes = -(-E // LANES) * LANES
    bf, f32 = jnp.bfloat16, jnp.float32
    pair = (2 * group, feats // (PATHS * PIECES))
    tile = (group, lanes)
    na, nb, nt = A - 1, B - 1, T - 1
    gather = S * 2 * (na + nb + nt + 1) + S * (nb + nt) + na + nb + 1
    scatter = S * 2 * (T + nb + nt + na) + 1 + nt + nb + na
    count = gather + scatter

    def vm(*shape, dtype=bf):
        return pltpu.VMEM(shape, dtype)

    scratch = [
        vm(width, hidden), vm(width, hidden), vm(hidden, width),
        vm(S, C, T, B, A, *pair), vm(S, C, B, T, A, *pair), vm(C, B, A, *tile, dtype=f32),
        vm(rows, width), vm(rows, width),
        vm(rows, hidden), vm(rows, hidden), vm(rows, hidden),
        vm(rows, hidden, dtype=f32), vm(rows, hidden, dtype=f32), vm(rows, hidden, dtype=f32),
        vm(S, C, T, B, A, *pair), vm(S, C, T, B, A, *pair),
        vm(S, T, B, A, *pair), vm(S, T, B, A, *pair),
        vm(S, T, B, A, *pair), vm(S, B, T, A, *pair),
        vm(S, nt, B, A, *pair), vm(S, nb, T, A, *pair),
        vm(S, B, A, *pair), vm(S, T, A, *pair),
        vm(S, nb, A, *pair), vm(S, nt, A, *pair),
        vm(S, A, *pair), vm(S, A, *pair),
        vm(S, na, *pair), vm(S, na, *pair),
        vm(C, B, A, *tile, dtype=f32), vm(B, A, *tile, dtype=f32),
        vm(T, B, A, *tile, dtype=f32), vm(B, A, *tile, dtype=f32),
        vm(nb, A, *tile, dtype=f32), vm(A, *tile, dtype=f32),
        vm(na, *tile, dtype=f32),
        pltpu.SemaphoreType.DMA((3,)),
        pltpu.SemaphoreType.DMA((count,)),
        pltpu.SemaphoreType.DMA((count,)),
    ]
    inside = pl.BlockSpec(memory_space=pltpu.VMEM)
    outside = pl.BlockSpec(memory_space=pl.ANY)
    shapes = (
        jax.ShapeDtypeStruct((group, feats), bf),
        jax.ShapeDtypeStruct((group, feats), bf),
        jax.ShapeDtypeStruct(expert_ids.shape, f32),
    )
    results = pl.pallas_call(
        functools.partial(kernel, A, B, T, count),
        out_shape=shapes,
        in_specs=[inside] * 4 + [outside] * 3,
        out_specs=(inside, inside, inside),
        scratch_shapes=scratch,
        compiler_params=pltpu.CompilerParams(
            collective_id=0, has_side_effects=True, vmem_limit_bytes=60 * 1024 * 1024
        ),
        cost_estimate=pl.CostEstimate(
            flops=12 * rows * width * hidden,
            bytes_accessed=6 * width * hidden,
            transcendentals=rows * hidden,
        ),
    )(tokens, out_grad, expert_ids, gate_probs, w_gate, w_up, w_down)
    return pl.pallas_call(
        settle, out_shape=shapes, in_specs=[inside] * 3, out_specs=(inside, inside, inside)
    )(*results)


def solution(mesh):
    placed = (
        P("expert", "tensor"),
        P("expert", "tensor"),
        P("expert", None),
        P("expert", None),
        P("expert", None, "tensor"),
        P("expert", None, "tensor"),
        P("expert", "tensor", None),
    )
    return jax.shard_map(
        per_device,
        mesh=mesh,
        in_specs=placed,
        out_specs=(P("expert", "tensor"), P("expert", "tensor"), P("expert", None)),
        check_vma=False,
    )
```

```python
import functools

import jax
import jax.numpy as jnp
from jax import lax
from jax.experimental import pallas as pl
from jax.experimental.pallas import tpu as pltpu
from jax.sharding import PartitionSpec as P

CORES = 2
LANES = 128
PATHS = 2
PIECES = 2
MESH = pl.DeviceIdType.MESH


def grid_of(expert_count):
    chips = expert_count // CORES
    fast = 1
    while (fast * 2) * (fast * 2) <= chips:
        fast *= 2
    return chips // fast, fast


def dot_nn(left, right):
    return jnp.dot(left, right, preferred_element_type=jnp.float32)


def dot_nt(left, right):
    return lax.dot_general(
        left, right, (((1,), (1,)), ((), ())), preferred_element_type=jnp.float32
    )


def kernel(
    A, B, T, count,
    tok_ref, grad_ref, ids_ref, prob_ref, wg_hbm, wu_hbm, wd_hbm,
    mixed_ref, tgrad_ref, pgrad_ref,
    wg, wu, wd, g0, g1, pg, xs, og, hid, gga, gup, sum_gate, sum_up, sum_back,
    r0, r1, rc0, rc1, s0, s1, rx0, ry1, u0, u1, ry0, rx1, v0, v1, rz0, rz1,
    qr, qc, qx, qt, qy, qv, qz,
    wsem, ssem, rsem,
):
    me = lax.axis_index("expert")
    t = lax.axis_index("tensor")
    c = lax.rem(me, CORES)
    b = lax.rem(lax.div(me, CORES), B)
    a = lax.div(me, CORES * B)
    group, feats = tok_ref.shape
    piece = feats // (PATHS * PIECES)
    lanes = pg.shape[-1]
    rows = xs.shape[0]
    pieces = range(PIECES)

    def spot(aa, bb, cc, tt):
        return ((aa * B + bb) * CORES + cc, tt)

    def turn(value, r, size):
        return lax.rem(value + r, size)

    def column(h, s):
        return (s * PATHS + h) * piece

    to_a = [spot(turn(a, r, A), b, c, t) for r in range(1, A)]
    to_b = [spot(a, turn(b, r, B), c, t) for r in range(1, B)]
    to_t = [spot(a, b, c, turn(t, r, T)) for r in range(1, T)]
    to_c = spot(a, b, 1 - c, t)

    loads = [
        pltpu.make_async_copy(src.at[0], dst, wsem.at[i])
        for i, (src, dst) in enumerate(((wg_hbm, wg), (wu_hbm, wu), (wd_hbm, wd)))
    ]

    barrier = pltpu.get_barrier_semaphore()
    peers = to_a + to_b + to_t + [to_c]
    for peer in peers:
        pl.semaphore_signal(barrier, inc=1, device_id=peer, device_id_type=MESH)
    for load in loads:
        load.start()

    ids = ids_ref[...]
    probs = prob_ref[...]
    lane = lax.broadcasted_iota(jnp.int32, (group, lanes), 1)
    routed = jnp.zeros((group, lanes), jnp.float32)
    for k in range(ids.shape[1]):
        routed = routed + jnp.where(lane == ids[:, k : k + 1], probs[:, k : k + 1], 0.0)
    unit = jnp.concatenate(
        [tok_ref[...].astype(jnp.float32), grad_ref[...].astype(jnp.float32)], axis=0
    ).astype(jnp.bfloat16)
    for s in pieces:
        g0[s, c, t, b, a] = unit[:, column(0, s) : column(0, s) + piece]
        g1[s, c, b, t, a] = unit[:, column(1, s) : column(1, s) + piece]
    pg[c, b, a] = routed
    pl.semaphore_wait(barrier, len(peers))

    started = []

    def send(src, dst, peer):
        i = len(started)
        copy = pltpu.make_async_remote_copy(
            src_ref=src, dst_ref=dst, send_sem=ssem.at[i], recv_sem=rsem.at[i],
            device_id=peer, device_id_type=MESH,
        )
        copy.start()
        started.append(copy)
        return copy

    def same(ref, peers):
        return [send(ref, ref, peer) for peer in peers]

    def arrive(copies):
        for copy in copies:
            copy.wait_recv()

    a0, a1, b0, b1, c0, c1 = ([None] * PIECES for _ in range(6))
    for s in pieces:
        a0[s] = same(g0.at[s, c, t, b, a], to_a)
        a1[s] = same(g1.at[s, c, b, t, a], to_a)
    ap = same(pg.at[c, b, a], to_a)
    for s in pieces:
        arrive(a0[s])
        b0[s] = same(g0.at[s, c, t, b], to_b)
        arrive(a1[s])
        b1[s] = same(g1.at[s, c, b, t], to_t)
    arrive(ap)
    bp = same(pg.at[c, b], to_b)
    own, rest0, rest1 = [], [], []
    for s in pieces:
        arrive(b0[s])
        c0[s] = same(g0.at[s, c, t], to_t)
        own += same(g0.at[s, c, t], [to_c])
        arrive(b1[s])
        c1[s] = same(g1.at[s, c, b], to_b)
        rest1.append(same(g1.at[s, c, b], [to_c]))
    arrive(bp)
    dp = same(pg.at[c], [to_c])

    part = B * A * group
    step = min(rows, 256)

    def assemble(slot, h, s, r):
        tt = turn(t, r, T)
        for cc in range(CORES):
            block = g0[s, cc, tt] if h == 0 else g1[s, cc, :, tt]
            block = block.astype(jnp.float32)
            at = (pl.ds(cc * part, part), pl.ds(slot * piece, piece))
            xs[at] = block[:, :, :group].reshape(part, piece).astype(jnp.bfloat16)
            og[at] = block[:, :, group:].reshape(part, piece).astype(jnp.bfloat16)

    def products(at, runs):
        gate = up = back = None
        for slot, h, s, r, width in runs:
            start = pl.multiple_of(turn(t, r, T) * feats + column(h, s), piece)
            here = pl.ds(slot * piece, width * piece)
            there = pl.ds(start, width * piece)
            x, o = xs[at, here], og[at, here]
            terms = dot_nn(x, wg[there, :]), dot_nn(x, wu[there, :]), dot_nt(wd[:, there], o)
            if gate is None:
                gate, up, back = terms
            else:
                gate, up, back = gate + terms[0], up + terms[1], back + terms[2]
        return gate, up, back

    def by_rows(body):
        if rows == step:
            body(pl.ds(0, rows))
        else:

            @pl.loop(0, rows // step)
            def _(i):
                body(pl.ds(pl.multiple_of(i * step, step), step))

    slots = 0

    def plan(runs):
        nonlocal slots
        out = []
        for h, s, r, width in runs:
            for i in range(width):
                assemble(slots + i, h + i, s, r)
            out.append((slots, h, s, r, width))
            slots += width
        return out

    def forward0(s):
        for r in range(1, T):
            c0[s][r - 1].wait_recv()
            rest0.append(same(g0.at[s, c, turn(t, T - r, T)], [to_c]))

    def forward1(s):
        for r in range(1, B):
            c1[s][r - 1].wait_recv()
            rest1.append(same(g1.at[s, c, turn(b, B - r, B)], [to_c]))

    forward0(0)
    for load in loads:
        load.wait()
    arrive(own)
    runs = plan([(0, s, 0, 1) for s in pieces])

    def begin(at):
        sum_gate[at, :], sum_up[at, :], sum_back[:, at] = products(at, runs)

    by_rows(begin)
    for s in pieces:
        forward1(s)
        if s:
            forward0(s)
    for copies in rest0 + rest1:
        arrive(copies)
    arrive(dp)
    more = plan(
        [(0, s, r, 2) for s in pieces for r in range(1, T)] + [(1, s, 0, 1) for s in pieces]
    )

    def finish(at):
        gate, up, back = products(at, more)
        gate = gate + sum_gate[at, :]
        up = up + sum_up[at, :]
        back = (back + sum_back[:, at]).T
        weights = pg.reshape(rows, lanes)[at, :]
        mine = lax.broadcasted_iota(jnp.int32, (step, lanes), 1) == me
        weight = jnp.sum(jnp.where(mine, weights, 0.0), axis=1, keepdims=True)
        sig = jax.nn.sigmoid(gate)
        silu = gate * sig
        hidden = silu * up
        inner = jnp.sum(hidden * back, axis=1, keepdims=True)
        back = back * weight
        hid[at, :] = (hidden * weight).astype(jnp.bfloat16)
        gga[at, :] = (back * up * sig * (1.0 + gate * (1.0 - sig))).astype(jnp.bfloat16)
        gup[at, :] = (back * silu).astype(jnp.bfloat16)
        qr.reshape(rows, lanes)[at, :] = jnp.where(mine, inner, 0.0)

    by_rows(finish)
    ec = send(qr.at[1 - c], qc, to_c)

    cuts = CORES if rows > 256 else 1

    def second(h, s, r):
        tt = turn(t, r, T)
        ref, landing = ((r0, rc0), (r1, rc1))[h]
        cols = pl.ds(pl.multiple_of(tt * feats + column(h, s), piece), piece)
        size = rows // cuts
        for i in range(cuts):
            at = pl.ds(i * size, size)
            out = dot_nn(hid[at, :], wd[:, cols])
            back = (dot_nt(wg[cols, :], gga[at, :]) + dot_nt(wu[cols, :], gup[at, :])).T
            shape = (CORES // cuts, B, A, group, piece)
            block = jnp.concatenate([out.reshape(shape), back.reshape(shape)], axis=3)
            block = block.astype(jnp.bfloat16)
            for j in range(CORES // cuts):
                ref[s, i + j, tt] = block[j]
        return send(ref.at[s, 1 - c, tt], landing.at[s, tt], to_c)

    def wide(value):
        return value.astype(jnp.float32)

    def narrow(value):
        return value.astype(jnp.bfloat16)

    def total(first_term, ref):
        value = wide(first_term)
        for i in range(ref.shape[0]):
            value = value + wide(ref[i])
        return value

    far = list(range(1, T))
    e0 = [[None] * T for _ in pieces]
    e1 = [[None] * T for _ in pieces]
    f0, f1, h0, h1, k0, k1 = ([None] * PIECES for _ in range(6))

    def away0(s):
        f0[s] = []
        for r in far:
            e0[s][r].wait_recv()
            tt = turn(t, r, T)
            s0[s, tt] = narrow(wide(r0[s, c, tt]) + wide(rc0[s, tt]))
            f0[s].append(send(s0.at[s, tt], rx0.at[s, r - 1], to_t[r - 1]))

    def home0(s):
        e0[s][0].wait_recv()
        s0[s, t] = narrow(wide(r0[s, c, t]) + wide(rc0[s, t]))

    def away1(s):
        arrive(e1[s])
        f1[s] = []
        for r in list(range(1, B)) + [0]:
            bb = turn(b, r, B)
            s1[s, bb] = narrow(wide(r1[s, c, :, bb]) + wide(rc1[s, :, bb]))
            if r:
                f1[s].append(send(s1.at[s, bb], ry1.at[s, r - 1], to_b[r - 1]))

    def across0(s):
        arrive(f0[s])
        u0[s] = narrow(total(s0[s, t], rx0.at[s]))
        h0[s] = [
            send(u0.at[s, turn(b, r, B)], ry0.at[s, r - 1], to_b[r - 1]) for r in range(1, B)
        ]

    def across1(s):
        arrive(f1[s])
        u1[s] = narrow(total(s1[s, b], ry1.at[s]))
        h1[s] = [
            send(u1.at[s, turn(t, r, T)], rx1.at[s, r - 1], to_t[r - 1]) for r in range(1, T)
        ]

    def along0(s):
        arrive(h0[s])
        v0[s] = narrow(total(u0[s, b], ry0.at[s]))
        k0[s] = [
            send(v0.at[s, turn(a, r, A)], rz0.at[s, r - 1], to_a[r - 1]) for r in range(1, A)
        ]

    def along1(s):
        arrive(h1[s])
        v1[s] = narrow(total(u1[s, t], rx1.at[s]))
        k1[s] = [
            send(v1.at[s, turn(a, r, A)], rz1.at[s, r - 1], to_a[r - 1]) for r in range(1, A)
        ]

    for s in pieces:
        for r in far:
            e0[s][r] = second(0, s, r)
        if s:
            home0(s - 1)
        for r in far:
            e1[s][r] = second(1, s, r)
        away0(s)
        if s:
            across0(s - 1)
        else:
            ec.wait_recv()
            qx[t] = qr[c] + qc[...]
            fq = same(qx.at[t], to_t)
        e1[s][0] = second(1, s, 0)
        e0[s][0] = second(0, s, 0)
        away1(s)
    last = PIECES - 1
    for s in range(last):
        across1(s)
    home0(last)
    arrive(fq)
    value = qx[0]
    for i in range(1, T):
        value = value + qx[i]
    qt[...] = value
    hq = [send(qt.at[turn(b, r, B)], qy.at[r - 1], to_b[r - 1]) for r in range(1, B)]
    for s in range(last):
        along0(s)
    across0(last)
    arrive(hq)
    qv[...] = total(qt[b], qy)
    kq = [send(qv.at[turn(a, r, A)], qz.at[r - 1], to_a[r - 1]) for r in range(1, A)]
    for s in range(last):
        along1(s)
    across1(last)
    along0(last)

    def deliver(h, s, mine, ref, copies):
        arrive(copies)
        value = total(mine, ref)
        at = pl.ds(column(h, s), piece)
        mixed_ref[:, at] = narrow(value[:group])
        tgrad_ref[:, at] = narrow(value[group:])

    for s in range(last):
        deliver(0, s, v0[s, a], rz0.at[s], k0[s])
    arrive(kq)
    inner = total(qv[a], qz)
    place = lax.broadcasted_iota(jnp.int32, ids.shape, 1)
    result = jnp.zeros(ids.shape, jnp.float32)
    for k in range(ids.shape[1]):
        one = jnp.sum(jnp.where(lane == ids[:, k : k + 1], inner, 0.0), axis=1, keepdims=True)
        result = jnp.where(place == k, one, result)
    pgrad_ref[...] = result
    along1(last)
    for s in range(last):
        deliver(1, s, v1[s, a], rz1.at[s], k1[s])
    deliver(0, last, v0[last, a], rz0.at[last], k0[last])
    deliver(1, last, v1[last, a], rz1.at[last], k1[last])
    assert len(started) == count
    for copy in started:
        copy.wait_send()


def settle(*refs):
    for source, target in zip(refs[: len(refs) // 2], refs[len(refs) // 2 :]):
        target[...] = source[...]


def per_device(tokens, out_grad, expert_ids, gate_probs, w_gate, w_up, w_down):
    E = lax.axis_size("expert")
    T = lax.axis_size("tensor")
    A, B = grid_of(E)
    C, S = CORES, PIECES
    group, feats = tokens.shape
    width = feats * T
    hidden = w_gate.shape[2]
    rows = E * group
    lanes = -(-E // LANES) * LANES
    bf, f32 = jnp.bfloat16, jnp.float32
    pair = (2 * group, feats // (PATHS * PIECES))
    tile = (group, lanes)
    na, nb, nt = A - 1, B - 1, T - 1
    gather = S * 2 * (na + nb + nt + 1) + S * (nb + nt) + na + nb + 1
    scatter = S * 2 * (T + nb + nt + na) + 1 + nt + nb + na
    count = gather + scatter

    def vm(*shape, dtype=bf):
        return pltpu.VMEM(shape, dtype)

    scratch = [
        vm(width, hidden), vm(width, hidden), vm(hidden, width),
        vm(S, C, T, B, A, *pair), vm(S, C, B, T, A, *pair), vm(C, B, A, *tile, dtype=f32),
        vm(rows, width), vm(rows, width),
        vm(rows, hidden), vm(rows, hidden), vm(rows, hidden),
        vm(rows, hidden, dtype=f32), vm(rows, hidden, dtype=f32), vm(hidden, rows, dtype=f32),
        vm(S, C, T, B, A, *pair), vm(S, C, T, B, A, *pair),
        vm(S, T, B, A, *pair), vm(S, T, B, A, *pair),
        vm(S, T, B, A, *pair), vm(S, B, T, A, *pair),
        vm(S, nt, B, A, *pair), vm(S, nb, T, A, *pair),
        vm(S, B, A, *pair), vm(S, T, A, *pair),
        vm(S, nb, A, *pair), vm(S, nt, A, *pair),
        vm(S, A, *pair), vm(S, A, *pair),
        vm(S, na, *pair), vm(S, na, *pair),
        vm(C, B, A, *tile, dtype=f32), vm(B, A, *tile, dtype=f32),
        vm(T, B, A, *tile, dtype=f32), vm(B, A, *tile, dtype=f32),
        vm(nb, A, *tile, dtype=f32), vm(A, *tile, dtype=f32),
        vm(na, *tile, dtype=f32),
        pltpu.SemaphoreType.DMA((3,)),
        pltpu.SemaphoreType.DMA((count,)),
        pltpu.SemaphoreType.DMA((count,)),
    ]
    inside = pl.BlockSpec(memory_space=pltpu.VMEM)
    outside = pl.BlockSpec(memory_space=pl.ANY)
    shapes = (
        jax.ShapeDtypeStruct((group, feats), bf),
        jax.ShapeDtypeStruct((group, feats), bf),
        jax.ShapeDtypeStruct(expert_ids.shape, f32),
    )
    results = pl.pallas_call(
        functools.partial(kernel, A, B, T, count),
        out_shape=shapes,
        in_specs=[inside] * 4 + [outside] * 3,
        out_specs=(inside, inside, inside),
        scratch_shapes=scratch,
        compiler_params=pltpu.CompilerParams(
            collective_id=0, has_side_effects=True, vmem_limit_bytes=60 * 1024 * 1024
        ),
        cost_estimate=pl.CostEstimate(
            flops=12 * rows * width * hidden,
            bytes_accessed=6 * width * hidden,
            transcendentals=rows * hidden,
        ),
    )(tokens, out_grad, expert_ids, gate_probs, w_gate, w_up, w_down)
    return pl.pallas_call(
        settle, out_shape=shapes, in_specs=[inside] * 3, out_specs=(inside, inside, inside)
    )(*results)


def solution(mesh):
    placed = (
        P("expert", "tensor"),
        P("expert", "tensor"),
        P("expert", None),
        P("expert", None),
        P("expert", None, "tensor"),
        P("expert", None, "tensor"),
        P("expert", "tensor", None),
    )
    return jax.shard_map(
        per_device,
        mesh=mesh,
        in_specs=placed,
        out_specs=(P("expert", "tensor"), P("expert", "tensor"), P("expert", None)),
        check_vma=False,
    )
```

```python
import functools

import jax
import jax.numpy as jnp
from jax import lax
from jax.experimental import pallas as pl
from jax.experimental.pallas import tpu as pltpu
from jax.sharding import PartitionSpec as P

CORES = 2
LANES = 128
PATHS = 2
PIECES = 2
MESH = pl.DeviceIdType.MESH


def grid_of(expert_count):
    chips = expert_count // CORES
    fast = 1
    while (fast * 2) * (fast * 2) <= chips:
        fast *= 2
    return chips // fast, fast


def dot_nn(left, right):
    return jnp.dot(left, right, preferred_element_type=jnp.float32)


def dot_nt(left, right):
    return lax.dot_general(
        left, right, (((1,), (1,)), ((), ())), preferred_element_type=jnp.float32
    )


def kernel(
    A, B, T, count,
    tok_ref, grad_ref, ids_ref, prob_ref, wg_hbm, wu_hbm, wd_hbm,
    mixed_ref, tgrad_ref, pgrad_ref,
    wg, wu, wd, g0, g1, pg, xs, og, hid, gga, gup, sum_gate, sum_up, sum_back,
    rr, rc, s0, s1, rx0, ry1, u0, u1, ry0, rx1, v0, v1, rz0, rz1,
    qr, qc, qx, qt, qy, qv, qz,
    wsem, ssem, rsem, csend, crecv,
):
    me = lax.axis_index("expert")
    t = lax.axis_index("tensor")
    c = lax.rem(me, CORES)
    b = lax.rem(lax.div(me, CORES), B)
    a = lax.div(me, CORES * B)
    group, feats = tok_ref.shape
    piece = feats // (PATHS * PIECES)
    lanes = pg.shape[-1]
    rows = xs.shape[0]
    pieces = range(PIECES)

    def spot(aa, bb, cc, tt):
        return ((aa * B + bb) * CORES + cc, tt)

    def turn(value, r, size):
        return lax.rem(value + r, size)

    def column(h, s):
        return (s * PATHS + h) * piece

    to_a = [spot(turn(a, r, A), b, c, t) for r in range(1, A)]
    to_b = [spot(a, turn(b, r, B), c, t) for r in range(1, B)]
    to_t = [spot(a, b, c, turn(t, r, T)) for r in range(1, T)]
    to_c = spot(a, b, 1 - c, t)

    loads = [
        pltpu.make_async_copy(src.at[0], dst, wsem.at[i])
        for i, (src, dst) in enumerate(((wg_hbm, wg), (wu_hbm, wu), (wd_hbm, wd)))
    ]

    barrier = pltpu.get_barrier_semaphore()
    peers = to_a + to_b + to_t + [to_c]
    for peer in peers:
        pl.semaphore_signal(barrier, inc=1, device_id=peer, device_id_type=MESH)
    for load in loads:
        load.start()

    ids = ids_ref[...]
    probs = prob_ref[...]
    lane = lax.broadcasted_iota(jnp.int32, (group, lanes), 1)
    routed = jnp.zeros((group, lanes), jnp.float32)
    for k in range(ids.shape[1]):
        routed = routed + jnp.where(lane == ids[:, k : k + 1], probs[:, k : k + 1], 0.0)
    unit = jnp.concatenate(
        [tok_ref[...].astype(jnp.float32), grad_ref[...].astype(jnp.float32)], axis=0
    ).astype(jnp.bfloat16)
    for s in pieces:
        g0[s, c, t, b, a] = unit[:, column(0, s) : column(0, s) + piece]
        g1[s, c, b, t, a] = unit[:, column(1, s) : column(1, s) + piece]
    pg[c, b, a] = routed
    pl.semaphore_wait(barrier, len(peers))

    started = []

    def view(part):
        return part[0].at[part[1]]

    def send(src, dst, peer):
        i = len(started)

        def copy():
            return pltpu.make_async_remote_copy(
                src_ref=view(src), dst_ref=view(dst), send_sem=ssem.at[i], recv_sem=rsem.at[i],
                device_id=peer, device_id_type=MESH,
            )

        copy().start()
        started.append(copy)
        return copy

    def same(ref, peers):
        return [send(ref, ref, peer) for peer in peers]

    def arrive(copies):
        for copy in copies:
            copy().wait_recv()

    a0, a1, b0, b1, c0, c1 = ([None] * PIECES for _ in range(6))
    for s in pieces:
        a0[s] = same((g0, (s, c, t, b, a,)), to_a)
        a1[s] = same((g1, (s, c, b, t, a,)), to_a)
    ap = same((pg, (c, b, a,)), to_a)
    for s in pieces:
        arrive(a0[s])
        b0[s] = same((g0, (s, c, t, b,)), to_b)
        arrive(a1[s])
        b1[s] = same((g1, (s, c, b, t,)), to_t)
    arrive(ap)
    bp = same((pg, (c, b,)), to_b)
    own, rest0, rest1 = [], [], []
    for s in pieces:
        arrive(b0[s])
        c0[s] = same((g0, (s, c, t,)), to_t)
        own += same((g0, (s, c, t,)), [to_c])
        arrive(b1[s])
        c1[s] = same((g1, (s, c, b,)), to_b)
        rest1.append(same((g1, (s, c, b,)), [to_c]))
    arrive(bp)
    dp = same((pg, (c,)), [to_c])

    part = B * A * group
    step = min(rows, 256)

    def assemble(slot, h, s, r):
        tt = turn(t, r, T)
        for cc in range(CORES):
            block = g0[s, cc, tt] if h == 0 else g1[s, cc, :, tt]
            block = block.astype(jnp.float32)
            at = (pl.ds(cc * part, part), pl.ds(slot * piece, piece))
            xs[at] = block[:, :, :group].reshape(part, piece).astype(jnp.bfloat16)
            og[at] = block[:, :, group:].reshape(part, piece).astype(jnp.bfloat16)

    wide_tile = 256 if hid.shape[1] % 256 == 0 else 128
    tiles = hid.shape[1] // wide_tile

    def tile_at(n):
        return pl.ds(pl.multiple_of(n * wide_tile, wide_tile), wide_tile)

    def products(at, runs, cols):
        gate = up = back = None
        for slot, start, width in runs:
            here = pl.ds(slot * piece, width * piece)
            there = pl.ds(start, width * piece)
            x, o = xs[at, here], og[at, here]
            terms = (
                dot_nn(x, wg[there, cols]), dot_nn(x, wu[there, cols]), dot_nt(o, wd[cols, there])
            )
            if gate is None:
                gate, up, back = terms
            else:
                gate, up, back = gate + terms[0], up + terms[1], back + terms[2]
        return gate, up, back

    def by_rows(body):
        if rows == step:
            body(pl.ds(0, rows))
        else:

            @pl.loop(0, rows // step)
            def _(i):
                body(pl.ds(pl.multiple_of(i * step, step), step))

    slots = 0

    def plan(runs):
        nonlocal slots
        out = []
        for h, s, r, width in runs:
            for i in range(width):
                assemble(slots + i, h + i, s, r)
            start = pl.multiple_of(turn(t, r, T) * feats + column(h, s), piece)
            out.append((slots, start, width))
            slots += width
        return out

    def forward0(s):
        for r in range(1, T):
            c0[s][r - 1]().wait_recv()
            rest0.append(same((g0, (s, c, turn(t, T - r, T),)), [to_c]))

    def forward1(s):
        for r in range(1, B):
            c1[s][r - 1]().wait_recv()
            rest1.append(same((g1, (s, c, turn(b, B - r, B),)), [to_c]))

    forward0(0)
    for load in loads:
        load.wait()
    arrive(own)
    runs = plan([(0, s, 0, 1) for s in pieces])

    def begin(at):
        @pl.loop(0, tiles)
        def _(n):
            cols = tile_at(n)
            sum_gate[at, cols], sum_up[at, cols], sum_back[at, cols] = products(at, runs, cols)

    by_rows(begin)
    for s in pieces:
        forward1(s)
        if s:
            forward0(s)
    for copies in rest0 + rest1:
        arrive(copies)
    arrive(dp)
    more = plan(
        [(0, s, r, 2) for s in pieces for r in range(1, T)] + [(1, s, 0, 1) for s in pieces]
    )

    def finish(at):
        weights = pg.reshape(rows, lanes)[at, :]
        mine = lax.broadcasted_iota(jnp.int32, (step, lanes), 1) == me
        weight = jnp.sum(jnp.where(mine, weights, 0.0), axis=1, keepdims=True)

        def tile(n, inner):
            cols = tile_at(n)
            gate, up, back = products(at, more, cols)
            gate = gate + sum_gate[at, cols]
            up = up + sum_up[at, cols]
            back = back + sum_back[at, cols]
            sig = jax.nn.sigmoid(gate)
            silu = gate * sig
            hidden = silu * up
            inner = inner + jnp.sum(hidden * back, axis=1, keepdims=True)
            back = back * weight
            hid[at, cols] = (hidden * weight).astype(jnp.bfloat16)
            gga[at, cols] = (back * up * sig * (1.0 + gate * (1.0 - sig))).astype(jnp.bfloat16)
            gup[at, cols] = (back * silu).astype(jnp.bfloat16)
            return inner

        inner = lax.fori_loop(0, tiles, tile, jnp.zeros((step, 1), jnp.float32))
        qr.reshape(rows, lanes)[at, :] = jnp.where(mine, inner, 0.0)

    by_rows(finish)
    ec = send((qr, (1 - c,)), (qc, ()), to_c)

    cuts = CORES if rows > 256 else 1

    blocks = PATHS * T * PIECES
    tts = [turn(t, r, T) for r in range(T)]
    bbs = [turn(b, r, B) for r in range(B)]
    aas = [turn(a, r, A) for r in range(A)]

    def to_core(h, s, tt, q):
        return pltpu.make_async_remote_copy(
            src_ref=rr.at[h, s, 1 - c, tt], dst_ref=rc.at[h, s, tt],
            send_sem=csend.at[q], recv_sem=crecv.at[q],
            device_id=to_c, device_id_type=MESH,
        )

    def order(h, s, r):
        return (s * T + (r + T - 1) % T) * PATHS + h

    def second(q):
        h = lax.rem(q, PATHS)
        turns = lax.div(q, PATHS)
        s = lax.div(turns, T)
        tt = lax.rem(t + 1 + lax.rem(turns, T), T)
        start = tt * feats + (s * PATHS + h) * piece
        cols = pl.ds(pl.multiple_of(start, piece), piece)
        size = rows // cuts
        for i in range(cuts):
            at = pl.ds(i * size, size)
            out = dot_nn(hid[at, :], wd[:, cols])
            back = dot_nt(gga[at, :], wg[cols, :]) + dot_nt(gup[at, :], wu[cols, :])
            shape = (CORES // cuts, B, A, group, piece)
            block = jnp.concatenate([out.reshape(shape), back.reshape(shape)], axis=3)
            block = block.astype(jnp.bfloat16)
            for j in range(CORES // cuts):
                rr[h, s, i + j, tt] = block[j]
        to_core(h, s, tt, q).start()

    def core_came(h, s, r):
        to_core(h, s, tts[r], order(h, s, r)).wait_recv()

    def wide(value):
        return value.astype(jnp.float32)

    def narrow(value):
        return value.astype(jnp.bfloat16)

    def total(first_term, ref):
        value = wide(first_term)
        for i in range(ref.shape[0]):
            value = value + wide(ref[i])
        return value

    f0, f1, h0, h1, k0, k1 = ([None] * PIECES for _ in range(6))
    late = {}

    def away0(s):
        f0[s] = []
        for r in range(1, T):
            core_came(0, s, r)
            tt = tts[r]
            s0[s, tt] = narrow(wide(rr[0, s, c, tt]) + wide(rc[0, s, tt]))
            f0[s].append(send((s0, (s, tt,)), (rx0, (s, r - 1,)), to_t[r - 1]))

    def home0(s):
        core_came(0, s, 0)
        s0[s, t] = narrow(wide(rr[0, s, c, t]) + wide(rc[0, s, t]))

    def away1(s):
        for r in range(T):
            core_came(1, s, r)
        f1[s] = []
        for r in list(range(1, B)) + [0]:
            bb = bbs[r]
            s1[s, bb] = narrow(wide(rr[1, s, c, :, bb]) + wide(rc[1, s, :, bb]))
            if r:
                f1[s].append(send((s1, (s, bb,)), (ry1, (s, r - 1,)), to_b[r - 1]))

    def across0(s):
        arrive(f0[s])
        u0[s] = narrow(total(s0[s, t], rx0.at[s]))
        h0[s] = [send((u0, (s, bbs[r],)), (ry0, (s, r - 1,)), to_b[r - 1]) for r in range(1, B)]

    def across1(s):
        arrive(f1[s])
        u1[s] = narrow(total(s1[s, b], ry1.at[s]))
        h1[s] = [send((u1, (s, tts[r],)), (rx1, (s, r - 1,)), to_t[r - 1]) for r in range(1, T)]

    def along0(s):
        arrive(h0[s])
        v0[s] = narrow(total(u0[s, b], ry0.at[s]))
        k0[s] = [send((v0, (s, aas[r],)), (rz0, (s, r - 1,)), to_a[r - 1]) for r in range(1, A)]

    def along1(s):
        arrive(h1[s])
        v1[s] = narrow(total(u1[s, t], rx1.at[s]))
        k1[s] = [send((v1, (s, aas[r],)), (rz1, (s, r - 1,)), to_a[r - 1]) for r in range(1, A)]

    def inner0():
        ec().wait_recv()
        qx[t] = qr[c] + qc[...]
        late["t"] = same((qx, (t,)), to_t)

    def inner1():
        arrive(late["t"])
        value = qx[0]
        for i in range(1, T):
            value = value + qx[i]
        qt[...] = value
        late["b"] = [send((qt, (bbs[r],)), (qy, (r - 1,)), to_b[r - 1]) for r in range(1, B)]

    def inner2():
        arrive(late["b"])
        qv[...] = total(qt[b], qy)
        late["a"] = [send((qv, (aas[r],)), (qz, (r - 1,)), to_a[r - 1]) for r in range(1, A)]

    each = PATHS * T
    tasks = [(1, 0, inner0, ()), (each, 0, inner1, ()), (each + 2, 0, inner2, ())]
    for s in range(PIECES):
        base = s * each
        tasks.append((base + each - 2, 1, away0, (s,)))
        tasks.append((base + each, 2, away1, (s,)))
        tasks.append((base + each, 3, home0, (s,)))
        tasks.append((base + each + 1, 4, across0, (s,)))
        tasks.append((base + each + 2, 5, across1, (s,)))
        tasks.append((base + each + 3, 6, along0, (s,)))
        tasks.append((base + each + 4, 7, along1, (s,)))
    tasks.sort(key=lambda task: task[:2])

    @pl.loop(0, blocks)
    def _(q):
        second(q)
        for k in range(blocks):
            now = [task for task in tasks if task[0] == k]
            if now:

                @pl.when(q == k)
                def _():
                    for task in now:
                        task[2](*task[3])

    for task in tasks:
        if task[0] >= blocks:
            task[2](*task[3])
    last = PIECES - 1

    def deliver(h, s, mine, ref, copies):
        arrive(copies)
        value = total(mine, ref)
        at = pl.ds(column(h, s), piece)
        mixed_ref[:, at] = narrow(value[:group])
        tgrad_ref[:, at] = narrow(value[group:])

    for s in range(last):
        deliver(0, s, v0[s, a], rz0.at[s], k0[s])
    arrive(late["a"])
    inner = total(qv[a], qz)
    place = lax.broadcasted_iota(jnp.int32, ids.shape, 1)
    result = jnp.zeros(ids.shape, jnp.float32)
    for k in range(ids.shape[1]):
        one = jnp.sum(jnp.where(lane == ids[:, k : k + 1], inner, 0.0), axis=1, keepdims=True)
        result = jnp.where(place == k, one, result)
    pgrad_ref[...] = result
    for s in range(last):
        deliver(1, s, v1[s, a], rz1.at[s], k1[s])
    deliver(0, last, v0[last, a], rz0.at[last], k0[last])
    deliver(1, last, v1[last, a], rz1.at[last], k1[last])
    assert len(started) == count
    for copy in started:
        copy().wait_send()
    for s in pieces:
        for h in range(PATHS):
            for r in range(T):
                to_core(h, s, tts[r], order(h, s, r)).wait_send()


def settle(*refs):
    for source, target in zip(refs[: len(refs) // 2], refs[len(refs) // 2 :]):
        target[...] = source[...]


def per_device(tokens, out_grad, expert_ids, gate_probs, w_gate, w_up, w_down):
    E = lax.axis_size("expert")
    T = lax.axis_size("tensor")
    A, B = grid_of(E)
    C, S = CORES, PIECES
    group, feats = tokens.shape
    width = feats * T
    hidden = w_gate.shape[2]
    rows = E * group
    lanes = -(-E // LANES) * LANES
    bf, f32 = jnp.bfloat16, jnp.float32
    pair = (2 * group, feats // (PATHS * PIECES))
    tile = (group, lanes)
    na, nb, nt = A - 1, B - 1, T - 1
    gather = S * 2 * (na + nb + nt + 1) + S * (nb + nt) + na + nb + 1
    scatter = S * 2 * (nb + nt + na) + 1 + nt + nb + na
    count = gather + scatter

    def vm(*shape, dtype=bf):
        return pltpu.VMEM(shape, dtype)

    scratch = [
        vm(width, hidden), vm(width, hidden), vm(hidden, width),
        vm(S, C, T, B, A, *pair), vm(S, C, B, T, A, *pair), vm(C, B, A, *tile, dtype=f32),
        vm(rows, width), vm(rows, width),
        vm(rows, hidden), vm(rows, hidden), vm(rows, hidden),
        vm(rows, hidden, dtype=f32), vm(rows, hidden, dtype=f32), vm(rows, hidden, dtype=f32),
        vm(PATHS, S, C, T, B, A, *pair), vm(PATHS, S, T, B, A, *pair),
        vm(S, T, B, A, *pair), vm(S, B, T, A, *pair),
        vm(S, nt, B, A, *pair), vm(S, nb, T, A, *pair),
        vm(S, B, A, *pair), vm(S, T, A, *pair),
        vm(S, nb, A, *pair), vm(S, nt, A, *pair),
        vm(S, A, *pair), vm(S, A, *pair),
        vm(S, na, *pair), vm(S, na, *pair),
        vm(C, B, A, *tile, dtype=f32), vm(B, A, *tile, dtype=f32),
        vm(T, B, A, *tile, dtype=f32), vm(B, A, *tile, dtype=f32),
        vm(nb, A, *tile, dtype=f32), vm(A, *tile, dtype=f32),
        vm(na, *tile, dtype=f32),
        pltpu.SemaphoreType.DMA((3,)),
        pltpu.SemaphoreType.DMA((count,)),
        pltpu.SemaphoreType.DMA((count,)),
        pltpu.SemaphoreType.DMA((PATHS * S * T,)),
        pltpu.SemaphoreType.DMA((PATHS * S * T,)),
    ]
    inside = pl.BlockSpec(memory_space=pltpu.VMEM)
    outside = pl.BlockSpec(memory_space=pl.ANY)
    shapes = (
        jax.ShapeDtypeStruct((group, feats), bf),
        jax.ShapeDtypeStruct((group, feats), bf),
        jax.ShapeDtypeStruct(expert_ids.shape, f32),
    )
    results = pl.pallas_call(
        functools.partial(kernel, A, B, T, count),
        out_shape=shapes,
        in_specs=[inside] * 4 + [outside] * 3,
        out_specs=(inside, inside, inside),
        scratch_shapes=scratch,
        compiler_params=pltpu.CompilerParams(
            collective_id=0, has_side_effects=True, vmem_limit_bytes=60 * 1024 * 1024
        ),
        cost_estimate=pl.CostEstimate(
            flops=12 * rows * width * hidden,
            bytes_accessed=6 * width * hidden,
            transcendentals=rows * hidden,
        ),
    )(tokens, out_grad, expert_ids, gate_probs, w_gate, w_up, w_down)
    return pl.pallas_call(
        settle, out_shape=shapes, in_specs=[inside] * 3, out_specs=(inside, inside, inside)
    )(*results)


def solution(mesh):
    placed = (
        P("expert", "tensor"),
        P("expert", "tensor"),
        P("expert", None),
        P("expert", None),
        P("expert", None, "tensor"),
        P("expert", None, "tensor"),
        P("expert", "tensor", None),
    )
    return jax.shard_map(
        per_device,
        mesh=mesh,
        in_specs=placed,
        out_specs=(P("expert", "tensor"), P("expert", "tensor"), P("expert", None)),
        check_vma=False,
    )
```

```python
import functools

import jax
import jax.numpy as jnp
from jax import lax
from jax.experimental import pallas as pl
from jax.experimental.pallas import tpu as pltpu
from jax.sharding import PartitionSpec as P

CORES = 2
LANES = 128
PATHS = 2
PIECES = 1
MESH = pl.DeviceIdType.MESH


def grid_of(expert_count):
    chips = expert_count // CORES
    fast = 1
    while (fast * 2) * (fast * 2) <= chips:
        fast *= 2
    return chips // fast, fast


def dot_nn(left, right):
    return jnp.dot(left, right, preferred_element_type=jnp.float32)


def dot_nt(left, right):
    return lax.dot_general(
        left, right, (((1,), (1,)), ((), ())), preferred_element_type=jnp.float32
    )


def kernel(
    A, B, T, count,
    tok_ref, grad_ref, ids_ref, prob_ref, wg_hbm, wu_hbm, wd_hbm,
    mixed_ref, tgrad_ref, pgrad_ref,
    wg, wu, wd, g0, g1, pg, xs, og, hid, gga, gup, sum_gate, sum_up, sum_back,
    r0, r1, rc0, rc1, s0, s1, rx0, ry1, u0, u1, ry0, rx1, v0, v1, rz0, rz1,
    qr, qc, qx, qt, qy, qv, qz,
    wsem, ssem, rsem,
):
    me = lax.axis_index("expert")
    t = lax.axis_index("tensor")
    c = lax.rem(me, CORES)
    b = lax.rem(lax.div(me, CORES), B)
    a = lax.div(me, CORES * B)
    group, feats = tok_ref.shape
    piece = feats // (PATHS * PIECES)
    lanes = pg.shape[-1]
    rows = xs.shape[0]
    pieces = range(PIECES)

    def spot(aa, bb, cc, tt):
        return ((aa * B + bb) * CORES + cc, tt)

    def turn(value, r, size):
        return lax.rem(value + r, size)

    def column(h, s):
        return (s * PATHS + h) * piece

    to_a = [spot(turn(a, r, A), b, c, t) for r in range(1, A)]
    to_b = [spot(a, turn(b, r, B), c, t) for r in range(1, B)]
    to_t = [spot(a, b, c, turn(t, r, T)) for r in range(1, T)]
    to_c = spot(a, b, 1 - c, t)

    loads = [
        pltpu.make_async_copy(src.at[0], dst, wsem.at[i])
        for i, (src, dst) in enumerate(((wg_hbm, wg), (wu_hbm, wu), (wd_hbm, wd)))
    ]

    barrier = pltpu.get_barrier_semaphore()
    peers = to_a + to_b + to_t + [to_c]
    for peer in peers:
        pl.semaphore_signal(barrier, inc=1, device_id=peer, device_id_type=MESH)
    for load in loads:
        load.start()

    ids = ids_ref[...]
    probs = prob_ref[...]
    lane = lax.broadcasted_iota(jnp.int32, (group, lanes), 1)
    routed = jnp.zeros((group, lanes), jnp.float32)
    for k in range(ids.shape[1]):
        routed = routed + jnp.where(lane == ids[:, k : k + 1], probs[:, k : k + 1], 0.0)
    unit = jnp.concatenate(
        [tok_ref[...].astype(jnp.float32), grad_ref[...].astype(jnp.float32)], axis=0
    ).astype(jnp.bfloat16)
    for s in pieces:
        g0[s, c, t, b, a] = unit[:, column(0, s) : column(0, s) + piece]
        g1[s, c, b, t, a] = unit[:, column(1, s) : column(1, s) + piece]
    pg[c, b, a] = routed
    pl.semaphore_wait(barrier, len(peers))

    started = []

    def send(src, dst, peer):
        i = len(started)
        copy = pltpu.make_async_remote_copy(
            src_ref=src, dst_ref=dst, send_sem=ssem.at[i], recv_sem=rsem.at[i],
            device_id=peer, device_id_type=MESH,
        )
        copy.start()
        started.append(copy)
        return copy

    def same(ref, peers):
        return [send(ref, ref, peer) for peer in peers]

    def arrive(copies):
        for copy in copies:
            copy.wait_recv()

    a0, a1, b0, b1, c0, c1 = ([None] * PIECES for _ in range(6))
    for s in pieces:
        a0[s] = same(g0.at[s, c, t, b, a], to_a)
        a1[s] = same(g1.at[s, c, b, t, a], to_a)
    ap = same(pg.at[c, b, a], to_a)
    for s in pieces:
        arrive(a0[s])
        b0[s] = same(g0.at[s, c, t, b], to_b)
        arrive(a1[s])
        b1[s] = same(g1.at[s, c, b, t], to_t)
    arrive(ap)
    bp = same(pg.at[c, b], to_b)
    own, rest0, rest1 = [], [], []
    for s in pieces:
        arrive(b0[s])
        c0[s] = same(g0.at[s, c, t], to_t)
        own += same(g0.at[s, c, t], [to_c])
        arrive(b1[s])
        c1[s] = same(g1.at[s, c, b], to_b)
        rest1.append(same(g1.at[s, c, b], [to_c]))
    arrive(bp)
    dp = same(pg.at[c], [to_c])

    part = B * A * group
    step = min(rows, 256)

    def assemble(slot, h, s, r):
        tt = turn(t, r, T)
        for cc in range(CORES):
            block = g0[s, cc, tt] if h == 0 else g1[s, cc, :, tt]
            block = block.astype(jnp.float32)
            at = (pl.ds(cc * part, part), pl.ds(slot * piece, piece))
            xs[at] = block[:, :, :group].reshape(part, piece).astype(jnp.bfloat16)
            og[at] = block[:, :, group:].reshape(part, piece).astype(jnp.bfloat16)

    def products(at, runs):
        gate = up = back = None
        for slot, h, s, r, width in runs:
            start = pl.multiple_of(turn(t, r, T) * feats + column(h, s), piece)
            here = pl.ds(slot * piece, width * piece)
            there = pl.ds(start, width * piece)
            x, o = xs[at, here], og[at, here]
            terms = dot_nn(x, wg[there, :]), dot_nn(x, wu[there, :]), dot_nt(o, wd[:, there])
            if gate is None:
                gate, up, back = terms
            else:
                gate, up, back = gate + terms[0], up + terms[1], back + terms[2]
        return gate, up, back

    def by_rows(body):
        if rows == step:
            body(pl.ds(0, rows))
        else:

            @pl.loop(0, rows // step)
            def _(i):
                body(pl.ds(pl.multiple_of(i * step, step), step))

    slots = 0

    def plan(runs):
        nonlocal slots
        out = []
        for h, s, r, width in runs:
            for i in range(width):
                assemble(slots + i, h + i, s, r)
            out.append((slots, h, s, r, width))
            slots += width
        return out

    def forward0(s):
        for r in range(1, T):
            c0[s][r - 1].wait_recv()
            rest0.append(same(g0.at[s, c, turn(t, T - r, T)], [to_c]))

    def forward1(s):
        for r in range(1, B):
            c1[s][r - 1].wait_recv()
            rest1.append(same(g1.at[s, c, turn(b, B - r, B)], [to_c]))

    forward0(0)
    for load in loads:
        load.wait()
    arrive(own)
    runs = plan([(0, s, 0, 1) for s in pieces])

    def begin(at):
        sum_gate[at, :], sum_up[at, :], sum_back[at, :] = products(at, runs)

    by_rows(begin)
    for s in pieces:
        forward1(s)
        if s:
            forward0(s)
    for copies in rest0 + rest1:
        arrive(copies)
    arrive(dp)
    more = plan(
        [(0, s, r, 2) for s in pieces for r in range(1, T)] + [(1, s, 0, 1) for s in pieces]
    )

    def finish(at):
        gate, up, back = products(at, more)
        gate = gate + sum_gate[at, :]
        up = up + sum_up[at, :]
        back = back + sum_back[at, :]
        weights = pg.reshape(rows, lanes)[at, :]
        mine = lax.broadcasted_iota(jnp.int32, (step, lanes), 1) == me
        weight = jnp.sum(jnp.where(mine, weights, 0.0), axis=1, keepdims=True)
        sig = jax.nn.sigmoid(gate)
        silu = gate * sig
        hidden = silu * up
        inner = jnp.sum(hidden * back, axis=1, keepdims=True)
        back = back * weight
        hid[at, :] = (hidden * weight).astype(jnp.bfloat16)
        gga[at, :] = (back * up * sig * (1.0 + gate * (1.0 - sig))).astype(jnp.bfloat16)
        gup[at, :] = (back * silu).astype(jnp.bfloat16)
        qr.reshape(rows, lanes)[at, :] = jnp.where(mine, inner, 0.0)

    by_rows(finish)
    ec = send(qr.at[1 - c], qc, to_c)

    cuts = CORES if rows > 256 else 1

    def second(h, s, r):
        tt = turn(t, r, T)
        ref, landing = ((r0, rc0), (r1, rc1))[h]
        cols = pl.ds(pl.multiple_of(tt * feats + column(h, s), piece), piece)
        size = rows // cuts
        for i in range(cuts):
            at = pl.ds(i * size, size)
            out = dot_nn(hid[at, :], wd[:, cols])
            back = dot_nt(gga[at, :], wg[cols, :]) + dot_nt(gup[at, :], wu[cols, :])
            shape = (CORES // cuts, B, A, group, piece)
            block = jnp.concatenate([out.reshape(shape), back.reshape(shape)], axis=3)
            block = block.astype(jnp.bfloat16)
            for j in range(CORES // cuts):
                ref[s, i + j, tt] = block[j]
        return send(ref.at[s, 1 - c, tt], landing.at[s, tt], to_c)

    def wide(value):
        return value.astype(jnp.float32)

    def narrow(value):
        return value.astype(jnp.bfloat16)

    def total(first_term, ref):
        value = wide(first_term)
        for i in range(ref.shape[0]):
            value = value + wide(ref[i])
        return value

    far = list(range(1, T))
    e0 = [[None] * T for _ in pieces]
    e1 = [[None] * T for _ in pieces]
    f0, f1, h0, h1, k0, k1 = ([None] * PIECES for _ in range(6))

    def away0(s):
        f0[s] = []
        for r in far:
            e0[s][r].wait_recv()
            tt = turn(t, r, T)
            s0[s, tt] = narrow(wide(r0[s, c, tt]) + wide(rc0[s, tt]))
            f0[s].append(send(s0.at[s, tt], rx0.at[s, r - 1], to_t[r - 1]))

    def home0(s):
        e0[s][0].wait_recv()
        s0[s, t] = narrow(wide(r0[s, c, t]) + wide(rc0[s, t]))

    def away1(s):
        arrive(e1[s])
        f1[s] = []
        for r in list(range(1, B)) + [0]:
            bb = turn(b, r, B)
            s1[s, bb] = narrow(wide(r1[s, c, :, bb]) + wide(rc1[s, :, bb]))
            if r:
                f1[s].append(send(s1.at[s, bb], ry1.at[s, r - 1], to_b[r - 1]))

    def across0(s):
        arrive(f0[s])
        u0[s] = narrow(total(s0[s, t], rx0.at[s]))
        h0[s] = [
            send(u0.at[s, turn(b, r, B)], ry0.at[s, r - 1], to_b[r - 1]) for r in range(1, B)
        ]

    def across1(s):
        arrive(f1[s])
        u1[s] = narrow(total(s1[s, b], ry1.at[s]))
        h1[s] = [
            send(u1.at[s, turn(t, r, T)], rx1.at[s, r - 1], to_t[r - 1]) for r in range(1, T)
        ]

    def along0(s):
        arrive(h0[s])
        v0[s] = narrow(total(u0[s, b], ry0.at[s]))
        k0[s] = [
            send(v0.at[s, turn(a, r, A)], rz0.at[s, r - 1], to_a[r - 1]) for r in range(1, A)
        ]

    def along1(s):
        arrive(h1[s])
        v1[s] = narrow(total(u1[s, t], rx1.at[s]))
        k1[s] = [
            send(v1.at[s, turn(a, r, A)], rz1.at[s, r - 1], to_a[r - 1]) for r in range(1, A)
        ]

    for s in pieces:
        for r in far:
            e0[s][r] = second(0, s, r)
        if s:
            home0(s - 1)
        for r in far:
            e1[s][r] = second(1, s, r)
        away0(s)
        if s:
            across0(s - 1)
        else:
            ec.wait_recv()
            qx[t] = qr[c] + qc[...]
            fq = same(qx.at[t], to_t)
        e1[s][0] = second(1, s, 0)
        e0[s][0] = second(0, s, 0)
        away1(s)
    last = PIECES - 1
    for s in range(last):
        across1(s)
    home0(last)
    arrive(fq)
    value = qx[0]
    for i in range(1, T):
        value = value + qx[i]
    qt[...] = value
    hq = [send(qt.at[turn(b, r, B)], qy.at[r - 1], to_b[r - 1]) for r in range(1, B)]
    for s in range(last):
        along0(s)
    across0(last)
    arrive(hq)
    qv[...] = total(qt[b], qy)
    kq = [send(qv.at[turn(a, r, A)], qz.at[r - 1], to_a[r - 1]) for r in range(1, A)]
    for s in range(last):
        along1(s)
    across1(last)
    along0(last)

    def deliver(h, s, mine, ref, copies):
        arrive(copies)
        value = total(mine, ref)
        at = pl.ds(column(h, s), piece)
        mixed_ref[:, at] = narrow(value[:group])
        tgrad_ref[:, at] = narrow(value[group:])

    for s in range(last):
        deliver(0, s, v0[s, a], rz0.at[s], k0[s])
    arrive(kq)
    inner = total(qv[a], qz)
    place = lax.broadcasted_iota(jnp.int32, ids.shape, 1)
    result = jnp.zeros(ids.shape, jnp.float32)
    for k in range(ids.shape[1]):
        one = jnp.sum(jnp.where(lane == ids[:, k : k + 1], inner, 0.0), axis=1, keepdims=True)
        result = jnp.where(place == k, one, result)
    pgrad_ref[...] = result
    along1(last)
    for s in range(last):
        deliver(1, s, v1[s, a], rz1.at[s], k1[s])
    deliver(0, last, v0[last, a], rz0.at[last], k0[last])
    deliver(1, last, v1[last, a], rz1.at[last], k1[last])
    assert len(started) == count
    for copy in started:
        copy.wait_send()


def settle(*refs):
    for source, target in zip(refs[: len(refs) // 2], refs[len(refs) // 2 :]):
        target[...] = source[...]


def per_device(tokens, out_grad, expert_ids, gate_probs, w_gate, w_up, w_down):
    E = lax.axis_size("expert")
    T = lax.axis_size("tensor")
    A, B = grid_of(E)
    C, S = CORES, PIECES
    group, feats = tokens.shape
    width = feats * T
    hidden = w_gate.shape[2]
    rows = E * group
    lanes = -(-E // LANES) * LANES
    bf, f32 = jnp.bfloat16, jnp.float32
    pair = (2 * group, feats // (PATHS * PIECES))
    tile = (group, lanes)
    na, nb, nt = A - 1, B - 1, T - 1
    gather = S * 2 * (na + nb + nt + 1) + S * (nb + nt) + na + nb + 1
    scatter = S * 2 * (T + nb + nt + na) + 1 + nt + nb + na
    count = gather + scatter

    def vm(*shape, dtype=bf):
        return pltpu.VMEM(shape, dtype)

    scratch = [
        vm(width, hidden), vm(width, hidden), vm(hidden, width),
        vm(S, C, T, B, A, *pair), vm(S, C, B, T, A, *pair), vm(C, B, A, *tile, dtype=f32),
        vm(rows, width), vm(rows, width),
        vm(rows, hidden), vm(rows, hidden), vm(rows, hidden),
        vm(rows, hidden, dtype=f32), vm(rows, hidden, dtype=f32), vm(rows, hidden, dtype=f32),
        vm(S, C, T, B, A, *pair), vm(S, C, T, B, A, *pair),
        vm(S, T, B, A, *pair), vm(S, T, B, A, *pair),
        vm(S, T, B, A, *pair), vm(S, B, T, A, *pair),
        vm(S, nt, B, A, *pair), vm(S, nb, T, A, *pair),
        vm(S, B, A, *pair), vm(S, T, A, *pair),
        vm(S, nb, A, *pair), vm(S, nt, A, *pair),
        vm(S, A, *pair), vm(S, A, *pair),
        vm(S, na, *pair), vm(S, na, *pair),
        vm(C, B, A, *tile, dtype=f32), vm(B, A, *tile, dtype=f32),
        vm(T, B, A, *tile, dtype=f32), vm(B, A, *tile, dtype=f32),
        vm(nb, A, *tile, dtype=f32), vm(A, *tile, dtype=f32),
        vm(na, *tile, dtype=f32),
        pltpu.SemaphoreType.DMA((3,)),
        pltpu.SemaphoreType.DMA((count,)),
        pltpu.SemaphoreType.DMA((count,)),
    ]
    inside = pl.BlockSpec(memory_space=pltpu.VMEM)
    outside = pl.BlockSpec(memory_space=pl.ANY)
    shapes = (
        jax.ShapeDtypeStruct((group, feats), bf),
        jax.ShapeDtypeStruct((group, feats), bf),
        jax.ShapeDtypeStruct(expert_ids.shape, f32),
    )
    results = pl.pallas_call(
        functools.partial(kernel, A, B, T, count),
        out_shape=shapes,
        in_specs=[inside] * 4 + [outside] * 3,
        out_specs=(inside, inside, inside),
        scratch_shapes=scratch,
        compiler_params=pltpu.CompilerParams(
            collective_id=0, has_side_effects=True, vmem_limit_bytes=60 * 1024 * 1024
        ),
        cost_estimate=pl.CostEstimate(
            flops=12 * rows * width * hidden,
            bytes_accessed=6 * width * hidden,
            transcendentals=rows * hidden,
        ),
    )(tokens, out_grad, expert_ids, gate_probs, w_gate, w_up, w_down)
    return pl.pallas_call(
        settle, out_shape=shapes, in_specs=[inside] * 3, out_specs=(inside, inside, inside)
    )(*results)


def solution(mesh):
    placed = (
        P("expert", "tensor"),
        P("expert", "tensor"),
        P("expert", None),
        P("expert", None),
        P("expert", None, "tensor"),
        P("expert", None, "tensor"),
        P("expert", "tensor", None),
    )
    return jax.shard_map(
        per_device,
        mesh=mesh,
        in_specs=placed,
        out_specs=(P("expert", "tensor"), P("expert", "tensor"), P("expert", None)),
        check_vma=False,
    )
```

```python
import functools

import jax
import jax.numpy as jnp
from jax import lax
from jax.experimental import pallas as pl
from jax.experimental.pallas import tpu as pltpu
from jax.sharding import PartitionSpec as P

CORES = 2
LANES = 128
PIECES = 2
MESH = pl.DeviceIdType.MESH


def grid_of(expert_count):
    chips = expert_count // CORES
    fast = 1
    while (fast * 2) * (fast * 2) <= chips:
        fast *= 2
    return chips // fast, fast


def dot_nn(left, right):
    return jnp.dot(left, right, preferred_element_type=jnp.float32)


def dot_nt(left, right):
    return lax.dot_general(
        left, right, (((1,), (1,)), ((), ())), preferred_element_type=jnp.float32
    )


def kernel(
    A, B, T, count,
    tok_ref, grad_ref, ids_ref, prob_ref, wg_hbm, wu_hbm, wd_hbm,
    mixed_ref, tgrad_ref, pgrad_ref,
    wg, wu, wd, g, pg, xs, og, hid, gga, gup, sum_gate, sum_up, sum_back,
    parts, landed, sums, rq, v, rz, qr, qc, qx, qv, qz,
    wsem, ssem, rsem,
):
    me = lax.axis_index("expert")
    t = lax.axis_index("tensor")
    c = lax.rem(me, CORES)
    b = lax.rem(lax.div(me, CORES), B)
    a = lax.div(me, CORES * B)
    group, feats = tok_ref.shape
    piece = feats // PIECES
    lanes = pg.shape[-1]
    rows = xs.shape[0]
    pieces = range(PIECES)

    def spot(aa, bb, cc, tt):
        return ((aa * B + bb) * CORES + cc, tt)

    def turn(value, r, size):
        return lax.rem(value + r, size)

    q = t * B + b
    offsets = [(i, j) for i in range(T) for j in range(B) if i or j]
    to_a = [spot(turn(a, r, A), b, c, t) for r in range(1, A)]
    to_b = [spot(a, turn(b, r, B), c, t) for r in range(1, B)]
    to_q = [spot(a, turn(b, j, B), c, turn(t, i, T)) for i, j in offsets]
    to_c = spot(a, b, 1 - c, t)

    loads = [
        pltpu.make_async_copy(src.at[0], dst, wsem.at[i])
        for i, (src, dst) in enumerate(((wg_hbm, wg), (wu_hbm, wu), (wd_hbm, wd)))
    ]

    barrier = pltpu.get_barrier_semaphore()
    peers = to_a + to_q + [to_c]
    for peer in peers:
        pl.semaphore_signal(barrier, inc=1, device_id=peer, device_id_type=MESH)
    for load in loads:
        load.start()

    ids = ids_ref[...]
    probs = prob_ref[...]
    lane = lax.broadcasted_iota(jnp.int32, (group, lanes), 1)
    routed = jnp.zeros((group, lanes), jnp.float32)
    for k in range(ids.shape[1]):
        routed = routed + jnp.where(lane == ids[:, k : k + 1], probs[:, k : k + 1], 0.0)
    unit = jnp.concatenate(
        [tok_ref[...].astype(jnp.float32), grad_ref[...].astype(jnp.float32)], axis=0
    ).astype(jnp.bfloat16)
    for s in pieces:
        g[s, c, q, a] = unit[:, s * piece : (s + 1) * piece]
    pg[c, b, a] = routed
    pl.semaphore_wait(barrier, len(peers))

    started = []

    def send(src, dst, peer):
        i = len(started)
        copy = pltpu.make_async_remote_copy(
            src_ref=src, dst_ref=dst, send_sem=ssem.at[i], recv_sem=rsem.at[i],
            device_id=peer, device_id_type=MESH,
        )
        copy.start()
        started.append(copy)
        return copy

    def same(ref, peers):
        return [send(ref, ref, peer) for peer in peers]

    def arrive(copies):
        for copy in copies:
            copy.wait_recv()

    along = [same(g.at[s, c, q, a], to_a) for s in pieces]
    ap = same(pg.at[c, b, a], to_a)
    across = []
    for s in pieces:
        arrive(along[s])
        across.append(same(g.at[s, c, q], to_q))
    arrive(ap)
    bp = same(pg.at[c, b], to_b)

    part = B * A * group
    step = min(rows, 256)

    def assemble(s):
        for cc in range(CORES):
            for tt in range(T):
                block = g[s, cc, tt * B : (tt + 1) * B].astype(jnp.float32)
                at = (pl.ds(cc * part, part), pl.ds((s * T + tt) * piece, piece))
                xs[at] = block[:, :, :group].reshape(part, piece).astype(jnp.bfloat16)
                og[at] = block[:, :, group:].reshape(part, piece).astype(jnp.bfloat16)

    def products(at, s):
        gate = up = back = None
        for tt in range(T):
            here = pl.ds((s * T + tt) * piece, piece)
            there = pl.ds(tt * feats + s * piece, piece)
            x, o = xs[at, here], og[at, here]
            terms = dot_nn(x, wg[there, :]), dot_nn(x, wu[there, :]), dot_nt(o, wd[:, there])
            if gate is None:
                gate, up, back = terms
            else:
                gate, up, back = gate + terms[0], up + terms[1], back + terms[2]
        return gate, up, back

    def by_rows(body):
        if rows == step:
            body(pl.ds(0, rows))
        else:

            @pl.loop(0, rows // step)
            def _(i):
                body(pl.ds(pl.multiple_of(i * step, step), step))

    def swap(s):
        arrive(across[s])
        return same(g.at[s, c], [to_c])

    came = swap(0)
    arrive(bp)
    dp = same(pg.at[c], [to_c])
    for load in loads:
        load.wait()
    for s in pieces[:-1]:
        arrive(came)
        assemble(s)

        def add(at):
            gate, up, back = products(at, s)
            if s:
                gate = gate + sum_gate[at, :]
                up = up + sum_up[at, :]
                back = back + sum_back[at, :]
            sum_gate[at, :], sum_up[at, :], sum_back[at, :] = gate, up, back

        by_rows(add)
        came = swap(s + 1)
    last = PIECES - 1
    arrive(came)
    arrive(dp)
    assemble(last)

    def finish(at):
        gate, up, back = products(at, last)
        if last:
            gate = gate + sum_gate[at, :]
            up = up + sum_up[at, :]
            back = back + sum_back[at, :]
        weights = pg.reshape(rows, lanes)[at, :]
        mine = lax.broadcasted_iota(jnp.int32, (step, lanes), 1) == me
        weight = jnp.sum(jnp.where(mine, weights, 0.0), axis=1, keepdims=True)
        sig = jax.nn.sigmoid(gate)
        silu = gate * sig
        hidden = silu * up
        inner = jnp.sum(hidden * back, axis=1, keepdims=True)
        back = back * weight
        hid[at, :] = (hidden * weight).astype(jnp.bfloat16)
        gga[at, :] = (back * up * sig * (1.0 + gate * (1.0 - sig))).astype(jnp.bfloat16)
        gup[at, :] = (back * silu).astype(jnp.bfloat16)
        qr.reshape(rows, lanes)[at, :] = jnp.where(mine, inner, 0.0)

    by_rows(finish)
    ec = send(qr.at[1 - c], qc, to_c)

    cuts = CORES if rows > 256 else 1

    def second(s, r):
        tt = turn(t, r, T)
        cols = pl.ds(pl.multiple_of(tt * feats + s * piece, piece), piece)
        size = rows // cuts
        for i in range(cuts):
            at = pl.ds(i * size, size)
            out = dot_nn(hid[at, :], wd[:, cols])
            back = dot_nt(gga[at, :], wg[cols, :]) + dot_nt(gup[at, :], wu[cols, :])
            shape = (CORES // cuts, B, A, group, piece)
            block = jnp.concatenate([out.reshape(shape), back.reshape(shape)], axis=3)
            block = block.astype(jnp.bfloat16)
            for j in range(CORES // cuts):
                parts[s, i + j, tt] = block[j]
        return send(parts.at[s, 1 - c, tt], landed.at[s, tt], to_c)

    def wide(value):
        return value.astype(jnp.float32)

    def narrow(value):
        return value.astype(jnp.bfloat16)

    def total(first_term, ref):
        value = wide(first_term)
        for i in range(ref.shape[0]):
            value = value + wide(ref[i])
        return value

    turns = list(range(1, T)) + [0]
    hops = [[] for _ in pieces]
    ends = [None] * PIECES
    cores = {}

    def hop(s, r):
        cores[s, r].wait_recv()
        tt = turn(t, r, T)
        sums[s, tt] = narrow(wide(parts[s, c, tt]) + wide(landed[s, tt]))
        for i, (rt, rb) in enumerate(offsets):
            if rt == r:
                source = sums.at[s, tt, turn(b, rb, B)]
                hops[s].append(send(source, rq.at[s, i], to_q[i]))

    def home(s):
        arrive(hops[s])
        v[s] = narrow(total(sums[s, t, b], rq.at[s]))
        ends[s] = [
            send(v.at[s, turn(a, r, A)], rz.at[s, r - 1], to_a[r - 1]) for r in range(1, A)
        ]

    before = None
    for s in pieces:
        for r in turns:
            cores[s, r] = second(s, r)
            if before is not None:
                hop(*before)
            else:
                ec.wait_recv()
                qc[...] = qr[c] + qc[...]
                qx[q] = qc[b]
                eq = [
                    send(qc.at[turn(b, j, B)], qx.at[q], peer)
                    for (i, j), peer in zip(offsets, to_q)
                ]
            before = (s, r)
    hop(*before)
    arrive(eq)
    qv[...] = total(qx[0], qx.at[pl.ds(1, T * B - 1)])
    kq = [send(qv.at[turn(a, r, A)], qz.at[r - 1], to_a[r - 1]) for r in range(1, A)]
    for s in pieces:
        home(s)
    for copy in started:
        copy.wait_send()
    arrive(kq)
    inner = total(qv[a], qz)
    place = lax.broadcasted_iota(jnp.int32, ids.shape, 1)
    result = jnp.zeros(ids.shape, jnp.float32)
    for k in range(ids.shape[1]):
        one = jnp.sum(jnp.where(lane == ids[:, k : k + 1], inner, 0.0), axis=1, keepdims=True)
        result = jnp.where(place == k, one, result)
    pgrad_ref[...] = result
    for s in pieces:
        arrive(ends[s])
        value = total(v[s, a], rz.at[s])
        at = pl.ds(s * piece, piece)
        mixed_ref[:, at] = narrow(value[:group])
        tgrad_ref[:, at] = narrow(value[group:])
    assert len(started) == count


def settle(*refs):
    for source, target in zip(refs[: len(refs) // 2], refs[len(refs) // 2 :]):
        target[...] = source[...]


def per_device(tokens, out_grad, expert_ids, gate_probs, w_gate, w_up, w_down):
    E = lax.axis_size("expert")
    T = lax.axis_size("tensor")
    A, B = grid_of(E)
    C, S = CORES, PIECES
    group, feats = tokens.shape
    width = feats * T
    hidden = w_gate.shape[2]
    rows = E * group
    lanes = -(-E // LANES) * LANES
    bf, f32 = jnp.bfloat16, jnp.float32
    pair = (2 * group, feats // PIECES)
    tile = (group, lanes)
    na, nb, nq = A - 1, B - 1, T * B - 1
    gather = S * (na + nq + 1) + na + nb + 1
    scatter = S * (T + nq + na) + 1 + nq + na
    count = gather + scatter

    def vm(*shape, dtype=bf):
        return pltpu.VMEM(shape, dtype)

    scratch = [
        vm(width, hidden), vm(width, hidden), vm(hidden, width),
        vm(S, C, T * B, A, *pair), vm(C, B, A, *tile, dtype=f32),
        vm(rows, width), vm(rows, width),
        vm(rows, hidden), vm(rows, hidden), vm(rows, hidden),
        vm(rows, hidden, dtype=f32), vm(rows, hidden, dtype=f32), vm(rows, hidden, dtype=f32),
        vm(S, C, T, B, A, *pair), vm(S, T, B, A, *pair), vm(S, T, B, A, *pair),
        vm(S, nq, A, *pair), vm(S, A, *pair), vm(S, na, *pair),
        vm(C, B, A, *tile, dtype=f32), vm(B, A, *tile, dtype=f32),
        vm(T * B, A, *tile, dtype=f32), vm(A, *tile, dtype=f32), vm(na, *tile, dtype=f32),
        pltpu.SemaphoreType.DMA((3,)),
        pltpu.SemaphoreType.DMA((count,)),
        pltpu.SemaphoreType.DMA((count,)),
    ]
    inside = pl.BlockSpec(memory_space=pltpu.VMEM)
    outside = pl.BlockSpec(memory_space=pl.ANY)
    shapes = (
        jax.ShapeDtypeStruct((group, feats), bf),
        jax.ShapeDtypeStruct((group, feats), bf),
        jax.ShapeDtypeStruct(expert_ids.shape, f32),
    )
    results = pl.pallas_call(
        functools.partial(kernel, A, B, T, count),
        out_shape=shapes,
        in_specs=[inside] * 4 + [outside] * 3,
        out_specs=(inside, inside, inside),
        scratch_shapes=scratch,
        compiler_params=pltpu.CompilerParams(
            collective_id=0, has_side_effects=True, vmem_limit_bytes=60 * 1024 * 1024
        ),
        cost_estimate=pl.CostEstimate(
            flops=12 * rows * width * hidden,
            bytes_accessed=6 * width * hidden,
            transcendentals=rows * hidden,
        ),
    )(tokens, out_grad, expert_ids, gate_probs, w_gate, w_up, w_down)
    return pl.pallas_call(
        settle, out_shape=shapes, in_specs=[inside] * 3, out_specs=(inside, inside, inside)
    )(*results)


def solution(mesh):
    placed = (
        P("expert", "tensor"),
        P("expert", "tensor"),
        P("expert", None),
        P("expert", None),
        P("expert", None, "tensor"),
        P("expert", None, "tensor"),
        P("expert", "tensor", None),
    )
    return jax.shard_map(
        per_device,
        mesh=mesh,
        in_specs=placed,
        out_specs=(P("expert", "tensor"), P("expert", "tensor"), P("expert", None)),
        check_vma=False,
    )
```

```python
import functools

import jax
import jax.numpy as jnp
from jax import lax
from jax.experimental import pallas as pl
from jax.experimental.pallas import tpu as pltpu
from jax.sharding import PartitionSpec as P

CORES = 2
LANES = 128
PIECES = 2
MESH = pl.DeviceIdType.MESH


def grid_of(expert_count):
    chips = expert_count // CORES
    fast = 1
    while (fast * 2) * (fast * 2) <= chips:
        fast *= 2
    return chips // fast, fast


def dot_nn(left, right):
    return jnp.dot(left, right, preferred_element_type=jnp.float32)


def dot_nt(left, right):
    return lax.dot_general(
        left, right, (((1,), (1,)), ((), ())), preferred_element_type=jnp.float32
    )


def kernel(
    A, B, T, count,
    tok_hbm, grad_hbm, ids_hbm, prob_hbm, wg_hbm, wu_hbm, wd_hbm,
    mixed_ref, tgrad_ref, pgrad_ref,
    tok_ref, grad_ref, ids_ref, prob_ref, wg, wu, wd, g, pg, xs, og, hid, gga, gup, sum_gate, sum_up, sum_back,
    parts, landed, sums, rq, v, rz, qr, qc, qx, qv, qz,
    isem, wsem, ssem, rsem,
):
    me = lax.axis_index("expert")
    t = lax.axis_index("tensor")
    c = lax.rem(me, CORES)
    b = lax.rem(lax.div(me, CORES), B)
    a = lax.div(me, CORES * B)
    group, feats = tok_ref.shape
    piece = feats // PIECES
    lanes = pg.shape[-1]
    rows = xs.shape[0]
    pieces = range(PIECES)

    def spot(aa, bb, cc, tt):
        return ((aa * B + bb) * CORES + cc, tt)

    def turn(value, r, size):
        return lax.rem(value + r, size)

    q = t * B + b
    offsets = [(i, j) for i in range(T) for j in range(B) if i or j]
    to_a = [spot(turn(a, r, A), b, c, t) for r in range(1, A)]
    to_b = [spot(a, turn(b, r, B), c, t) for r in range(1, B)]
    to_q = [spot(a, turn(b, j, B), c, turn(t, i, T)) for i, j in offsets]
    to_c = spot(a, b, 1 - c, t)

    loads = [
        pltpu.make_async_copy(src.at[0], dst, wsem.at[i])
        for i, (src, dst) in enumerate(((wg_hbm, wg), (wu_hbm, wu), (wd_hbm, wd)))
    ]

    barrier = pltpu.get_barrier_semaphore()
    peers = to_a + to_q + [to_c]
    for peer in peers:
        pl.semaphore_signal(barrier, inc=1, device_id=peer, device_id_type=MESH)
    small = [
        pltpu.make_async_copy(src, dst, isem.at[i])
        for i, (src, dst) in enumerate(
            (
                (tok_hbm, tok_ref), (grad_hbm, grad_ref),
                (ids_hbm, ids_ref), (prob_hbm, prob_ref),
            )
        )
    ]
    for load in small + loads:
        load.start()
    for load in small:
        load.wait()

    ids = ids_ref[...]
    probs = prob_ref[...]
    lane = lax.broadcasted_iota(jnp.int32, (group, lanes), 1)
    routed = jnp.zeros((group, lanes), jnp.float32)
    for k in range(ids.shape[1]):
        routed = routed + jnp.where(lane == ids[:, k : k + 1], probs[:, k : k + 1], 0.0)
    unit = jnp.concatenate(
        [tok_ref[...].astype(jnp.float32), grad_ref[...].astype(jnp.float32)], axis=0
    ).astype(jnp.bfloat16)
    for s in pieces:
        g[s, c, q, a] = unit[:, s * piece : (s + 1) * piece]
    pg[c, b, a] = routed
    pl.semaphore_wait(barrier, len(peers))

    started = []

    def send(src, dst, peer):
        i = len(started)
        copy = pltpu.make_async_remote_copy(
            src_ref=src, dst_ref=dst, send_sem=ssem.at[i], recv_sem=rsem.at[i],
            device_id=peer, device_id_type=MESH,
        )
        copy.start()
        started.append(copy)
        return copy

    def same(ref, peers):
        return [send(ref, ref, peer) for peer in peers]

    def arrive(copies):
        for copy in copies:
            copy.wait_recv()

    along = [same(g.at[s, c, q, a], to_a) for s in pieces]
    ap = same(pg.at[c, b, a], to_a)
    across = []
    for s in pieces:
        arrive(along[s])
        across.append(same(g.at[s, c, q], to_q))
    arrive(ap)
    bp = same(pg.at[c, b], to_b)

    part = B * A * group
    step = min(rows, 256)

    def assemble(s):
        for cc in range(CORES):
            for tt in range(T):
                block = g[s, cc, tt * B : (tt + 1) * B].astype(jnp.float32)
                at = (pl.ds(cc * part, part), pl.ds((s * T + tt) * piece, piece))
                xs[at] = block[:, :, :group].reshape(part, piece).astype(jnp.bfloat16)
                og[at] = block[:, :, group:].reshape(part, piece).astype(jnp.bfloat16)

    def products(at, s):
        gate = up = back = None
        for tt in range(T):
            here = pl.ds((s * T + tt) * piece, piece)
            there = pl.ds(tt * feats + s * piece, piece)
            x, o = xs[at, here], og[at, here]
            terms = dot_nn(x, wg[there, :]), dot_nn(x, wu[there, :]), dot_nt(o, wd[:, there])
            if gate is None:
                gate, up, back = terms
            else:
                gate, up, back = gate + terms[0], up + terms[1], back + terms[2]
        return gate, up, back

    def by_rows(body):
        if rows == step:
            body(pl.ds(0, rows))
        else:

            @pl.loop(0, rows // step)
            def _(i):
                body(pl.ds(pl.multiple_of(i * step, step), step))

    def swap(s):
        arrive(across[s])
        return same(g.at[s, c], [to_c])

    came = swap(0)
    arrive(bp)
    dp = same(pg.at[c], [to_c])
    for load in loads:
        load.wait()
    for s in pieces[:-1]:
        arrive(came)
        assemble(s)

        def add(at):
            gate, up, back = products(at, s)
            if s:
                gate = gate + sum_gate[at, :]
                up = up + sum_up[at, :]
                back = back + sum_back[at, :]
            sum_gate[at, :], sum_up[at, :], sum_back[at, :] = gate, up, back

        by_rows(add)
        came = swap(s + 1)
    last = PIECES - 1
    arrive(came)
    arrive(dp)
    assemble(last)

    def finish(at):
        gate, up, back = products(at, last)
        if last:
            gate = gate + sum_gate[at, :]
            up = up + sum_up[at, :]
            back = back + sum_back[at, :]
        weights = pg.reshape(rows, lanes)[at, :]
        mine = lax.broadcasted_iota(jnp.int32, (step, lanes), 1) == me
        weight = jnp.sum(jnp.where(mine, weights, 0.0), axis=1, keepdims=True)
        sig = jax.nn.sigmoid(gate)
        silu = gate * sig
        hidden = silu * up
        inner = jnp.sum(hidden * back, axis=1, keepdims=True)
        back = back * weight
        hid[at, :] = (hidden * weight).astype(jnp.bfloat16)
        gga[at, :] = (back * up * sig * (1.0 + gate * (1.0 - sig))).astype(jnp.bfloat16)
        gup[at, :] = (back * silu).astype(jnp.bfloat16)
        qr.reshape(rows, lanes)[at, :] = jnp.where(mine, inner, 0.0)

    by_rows(finish)
    ec = send(qr.at[1 - c], qc, to_c)

    cuts = CORES if rows > 256 else 1

    def second(s, r):
        tt = turn(t, r, T)
        cols = pl.ds(pl.multiple_of(tt * feats + s * piece, piece), piece)
        size = rows // cuts
        for i in range(cuts):
            at = pl.ds(i * size, size)
            out = dot_nn(hid[at, :], wd[:, cols])
            back = dot_nt(gga[at, :], wg[cols, :]) + dot_nt(gup[at, :], wu[cols, :])
            shape = (CORES // cuts, B, A, group, piece)
            block = jnp.concatenate([out.reshape(shape), back.reshape(shape)], axis=3)
            block = block.astype(jnp.bfloat16)
            for j in range(CORES // cuts):
                parts[s, i + j, tt] = block[j]
        return send(parts.at[s, 1 - c, tt], landed.at[s, tt], to_c)

    def wide(value):
        return value.astype(jnp.float32)

    def narrow(value):
        return value.astype(jnp.bfloat16)

    def total(first_term, ref):
        value = wide(first_term)
        for i in range(ref.shape[0]):
            value = value + wide(ref[i])
        return value

    turns = list(range(1, T)) + [0]
    hops = [[] for _ in pieces]
    ends = [None] * PIECES
    cores = {}

    def hop(s, r):
        cores[s, r].wait_recv()
        tt = turn(t, r, T)
        sums[s, tt] = narrow(wide(parts[s, c, tt]) + wide(landed[s, tt]))
        for i, (rt, rb) in enumerate(offsets):
            if rt == r:
                source = sums.at[s, tt, turn(b, rb, B)]
                hops[s].append(send(source, rq.at[s, i], to_q[i]))

    def home(s):
        arrive(hops[s])
        v[s] = narrow(total(sums[s, t, b], rq.at[s]))
        ends[s] = [
            send(v.at[s, turn(a, r, A)], rz.at[s, r - 1], to_a[r - 1]) for r in range(1, A)
        ]

    before = None
    for s in pieces:
        for r in turns:
            cores[s, r] = second(s, r)
            if before is not None:
                hop(*before)
            else:
                ec.wait_recv()
                qc[...] = qr[c] + qc[...]
                qx[q] = qc[b]
                eq = [
                    send(qc.at[turn(b, j, B)], qx.at[q], peer)
                    for (i, j), peer in zip(offsets, to_q)
                ]
            before = (s, r)
    hop(*before)
    arrive(eq)
    qv[...] = total(qx[0], qx.at[pl.ds(1, T * B - 1)])
    kq = [send(qv.at[turn(a, r, A)], qz.at[r - 1], to_a[r - 1]) for r in range(1, A)]
    for s in pieces:
        home(s)
    for copy in started:
        copy.wait_send()
    arrive(kq)
    inner = total(qv[a], qz)
    place = lax.broadcasted_iota(jnp.int32, ids.shape, 1)
    result = jnp.zeros(ids.shape, jnp.float32)
    for k in range(ids.shape[1]):
        one = jnp.sum(jnp.where(lane == ids[:, k : k + 1], inner, 0.0), axis=1, keepdims=True)
        result = jnp.where(place == k, one, result)
    pgrad_ref[...] = result
    for s in pieces:
        arrive(ends[s])
        value = total(v[s, a], rz.at[s])
        at = pl.ds(s * piece, piece)
        mixed_ref[:, at] = narrow(value[:group])
        tgrad_ref[:, at] = narrow(value[group:])
    assert len(started) == count


def settle(*refs):
    *arrays, sem = refs
    count = len(arrays) // 2
    copies = [
        pltpu.make_async_copy(arrays[i], arrays[count + i], sem.at[i]) for i in range(count)
    ]
    for copy in copies:
        copy.start()
    for copy in copies:
        copy.wait()


def per_device(tokens, out_grad, expert_ids, gate_probs, w_gate, w_up, w_down):
    E = lax.axis_size("expert")
    T = lax.axis_size("tensor")
    A, B = grid_of(E)
    C, S = CORES, PIECES
    group, feats = tokens.shape
    width = feats * T
    hidden = w_gate.shape[2]
    rows = E * group
    lanes = -(-E // LANES) * LANES
    bf, f32 = jnp.bfloat16, jnp.float32
    pair = (2 * group, feats // PIECES)
    tile = (group, lanes)
    na, nb, nq = A - 1, B - 1, T * B - 1
    gather = S * (na + nq + 1) + na + nb + 1
    scatter = S * (T + nq + na) + 1 + nq + na
    count = gather + scatter

    def vm(*shape, dtype=bf):
        return pltpu.VMEM(shape, dtype)

    scratch = [
        vm(group, feats), vm(group, feats),
        vm(*expert_ids.shape, dtype=jnp.int32), vm(*gate_probs.shape, dtype=f32),
        vm(width, hidden), vm(width, hidden), vm(hidden, width),
        vm(S, C, T * B, A, *pair), vm(C, B, A, *tile, dtype=f32),
        vm(rows, width), vm(rows, width),
        vm(rows, hidden), vm(rows, hidden), vm(rows, hidden),
        vm(rows, hidden, dtype=f32), vm(rows, hidden, dtype=f32), vm(rows, hidden, dtype=f32),
        vm(S, C, T, B, A, *pair), vm(S, T, B, A, *pair), vm(S, T, B, A, *pair),
        vm(S, nq, A, *pair), vm(S, A, *pair), vm(S, na, *pair),
        vm(C, B, A, *tile, dtype=f32), vm(B, A, *tile, dtype=f32),
        vm(T * B, A, *tile, dtype=f32), vm(A, *tile, dtype=f32), vm(na, *tile, dtype=f32),
        pltpu.SemaphoreType.DMA((4,)),
        pltpu.SemaphoreType.DMA((3,)),
        pltpu.SemaphoreType.DMA((count,)),
        pltpu.SemaphoreType.DMA((count,)),
    ]
    inside = pl.BlockSpec(memory_space=pltpu.VMEM)
    outside = pl.BlockSpec(memory_space=pl.ANY)
    shapes = (
        jax.ShapeDtypeStruct((group, feats), bf),
        jax.ShapeDtypeStruct((group, feats), bf),
        jax.ShapeDtypeStruct(expert_ids.shape, f32),
    )
    results = pl.pallas_call(
        functools.partial(kernel, A, B, T, count),
        out_shape=shapes,
        in_specs=[outside] * 7,
        out_specs=(inside, inside, inside),
        scratch_shapes=scratch,
        compiler_params=pltpu.CompilerParams(
            collective_id=0, has_side_effects=True, vmem_limit_bytes=60 * 1024 * 1024
        ),
        cost_estimate=pl.CostEstimate(
            flops=12 * rows * width * hidden,
            bytes_accessed=6 * width * hidden,
            transcendentals=rows * hidden,
        ),
    )(tokens, out_grad, expert_ids, gate_probs, w_gate, w_up, w_down)
    return pl.pallas_call(
        settle,
        out_shape=shapes,
        in_specs=[outside] * 3,
        out_specs=(outside, outside, outside),
        scratch_shapes=[pltpu.SemaphoreType.DMA((3,))],
    )(*results)


def solution(mesh):
    placed = (
        P("expert", "tensor"),
        P("expert", "tensor"),
        P("expert", None),
        P("expert", None),
        P("expert", None, "tensor"),
        P("expert", None, "tensor"),
        P("expert", "tensor", None),
    )
    return jax.shard_map(
        per_device,
        mesh=mesh,
        in_specs=placed,
        out_specs=(P("expert", "tensor"), P("expert", "tensor"), P("expert", None)),
        check_vma=False,
    )
```

```python
import functools

import jax
import jax.numpy as jnp
from jax import lax
from jax.experimental import pallas as pl
from jax.experimental.pallas import tpu as pltpu
from jax.sharding import PartitionSpec as P

CORES = 2
LANES = 128
PIECES = 2
MESH = pl.DeviceIdType.MESH


def grid_of(expert_count):
    chips = expert_count // CORES
    fast = 1
    while (fast * 2) * (fast * 2) <= chips:
        fast *= 2
    return chips // fast, fast


def dot_nn(left, right):
    return jnp.dot(left, right, preferred_element_type=jnp.float32)


def dot_nt(left, right):
    return lax.dot_general(
        left, right, (((1,), (1,)), ((), ())), preferred_element_type=jnp.float32
    )


def kernel(
    A, B, T, count,
    tok_hbm, grad_hbm, ids_hbm, prob_hbm, wg_hbm, wu_hbm, wd_hbm,
    mixed_ref, tgrad_ref, pgrad_ref,
    tok_ref, grad_ref, ids_ref, prob_ref, wg, wu, wd, g, pg, xs, og, hid, gga, gup, sum_gate, sum_up, sum_back,
    parts, landed, sums, rq, v, rz, qr, qc, qx, qv, qz,
    isem, wsem, ssem, rsem,
):
    me = lax.axis_index("expert")
    t = lax.axis_index("tensor")
    c = lax.rem(me, CORES)
    b = lax.rem(lax.div(me, CORES), B)
    a = lax.div(me, CORES * B)
    group, feats = tok_ref.shape
    piece = feats // PIECES
    lanes = pg.shape[-1]
    rows = xs.shape[0]
    pieces = range(PIECES)

    def spot(aa, bb, cc, tt):
        return ((aa * B + bb) * CORES + cc, tt)

    def turn(value, r, size):
        return lax.rem(value + r, size)

    q = t * B + b
    offsets = [(i, j) for i in range(T) for j in range(B) if i or j][::-1]
    to_a = [spot(turn(a, r, A), b, c, t) for r in range(1, A)]
    to_b = [spot(a, turn(b, r, B), c, t) for r in range(1, B)]
    to_q = [spot(a, turn(b, j, B), c, turn(t, i, T)) for i, j in offsets]
    to_c = spot(a, b, 1 - c, t)

    loads = [
        pltpu.make_async_copy(src.at[0], dst, wsem.at[i])
        for i, (src, dst) in enumerate(((wg_hbm, wg), (wu_hbm, wu), (wd_hbm, wd)))
    ]

    barrier = pltpu.get_barrier_semaphore()
    peers = to_a + to_q + [to_c]
    for peer in peers:
        pl.semaphore_signal(barrier, inc=1, device_id=peer, device_id_type=MESH)
    small = [
        pltpu.make_async_copy(src, dst, isem.at[i])
        for i, (src, dst) in enumerate(
            (
                (tok_hbm, tok_ref), (grad_hbm, grad_ref),
                (ids_hbm, ids_ref), (prob_hbm, prob_ref),
            )
        )
    ]
    for load in small + loads:
        load.start()
    for load in small:
        load.wait()

    ids = ids_ref[...]
    probs = prob_ref[...]
    lane = lax.broadcasted_iota(jnp.int32, (group, lanes), 1)
    routed = jnp.zeros((group, lanes), jnp.float32)
    for k in range(ids.shape[1]):
        routed = routed + jnp.where(lane == ids[:, k : k + 1], probs[:, k : k + 1], 0.0)
    unit = jnp.concatenate(
        [tok_ref[...].astype(jnp.float32), grad_ref[...].astype(jnp.float32)], axis=0
    ).astype(jnp.bfloat16)
    for s in pieces:
        g[s, c, q, a] = unit[:, s * piece : (s + 1) * piece]
    pg[c, b, a] = routed
    pl.semaphore_wait(barrier, len(peers))

    started = []

    def send(src, dst, peer):
        i = len(started)
        copy = pltpu.make_async_remote_copy(
            src_ref=src, dst_ref=dst, send_sem=ssem.at[i], recv_sem=rsem.at[i],
            device_id=peer, device_id_type=MESH,
        )
        copy.start()
        started.append(copy)
        return copy

    def same(ref, peers):
        return [send(ref, ref, peer) for peer in peers]

    def arrive(copies):
        for copy in copies:
            copy.wait_recv()

    along = [same(g.at[s, c, q, a], to_a) for s in pieces]
    ap = same(pg.at[c, b, a], to_a)
    across = []
    for s in pieces:
        arrive(along[s])
        across.append(same(g.at[s, c, q], to_q))
    arrive(ap)
    bp = same(pg.at[c, b], to_b)

    part = B * A * group
    step = min(rows, 256)

    def assemble(s):
        for cc in range(CORES):
            for tt in range(T):
                block = g[s, cc, tt * B : (tt + 1) * B].astype(jnp.float32)
                at = (pl.ds(cc * part, part), pl.ds((s * T + tt) * piece, piece))
                xs[at] = block[:, :, :group].reshape(part, piece).astype(jnp.bfloat16)
                og[at] = block[:, :, group:].reshape(part, piece).astype(jnp.bfloat16)

    def products(at, s):
        gate = up = back = None
        for tt in range(T):
            here = pl.ds((s * T + tt) * piece, piece)
            there = pl.ds(tt * feats + s * piece, piece)
            x, o = xs[at, here], og[at, here]
            terms = dot_nn(x, wg[there, :]), dot_nn(x, wu[there, :]), dot_nt(o, wd[:, there])
            if gate is None:
                gate, up, back = terms
            else:
                gate, up, back = gate + terms[0], up + terms[1], back + terms[2]
        return gate, up, back

    def by_rows(body):
        if rows == step:
            body(pl.ds(0, rows))
        else:

            @pl.loop(0, rows // step)
            def _(i):
                body(pl.ds(pl.multiple_of(i * step, step), step))

    def swap(s):
        arrive(across[s])
        return same(g.at[s, c], [to_c])

    came = swap(0)
    arrive(bp)
    dp = same(pg.at[c], [to_c])
    for load in loads:
        load.wait()
    for s in pieces[:-1]:
        arrive(came)
        assemble(s)

        def add(at):
            gate, up, back = products(at, s)
            if s:
                gate = gate + sum_gate[at, :]
                up = up + sum_up[at, :]
                back = back + sum_back[at, :]
            sum_gate[at, :], sum_up[at, :], sum_back[at, :] = gate, up, back

        by_rows(add)
        came = swap(s + 1)
    last = PIECES - 1
    arrive(came)
    arrive(dp)
    assemble(last)

    def finish(at):
        gate, up, back = products(at, last)
        if last:
            gate = gate + sum_gate[at, :]
            up = up + sum_up[at, :]
            back = back + sum_back[at, :]
        weights = pg.reshape(rows, lanes)[at, :]
        mine = lax.broadcasted_iota(jnp.int32, (step, lanes), 1) == me
        weight = jnp.sum(jnp.where(mine, weights, 0.0), axis=1, keepdims=True)
        sig = jax.nn.sigmoid(gate)
        silu = gate * sig
        hidden = silu * up
        inner = jnp.sum(hidden * back, axis=1, keepdims=True)
        back = back * weight
        hid[at, :] = (hidden * weight).astype(jnp.bfloat16)
        gga[at, :] = (back * up * sig * (1.0 + gate * (1.0 - sig))).astype(jnp.bfloat16)
        gup[at, :] = (back * silu).astype(jnp.bfloat16)
        qr.reshape(rows, lanes)[at, :] = jnp.where(mine, inner, 0.0)

    by_rows(finish)
    ec = send(qr.at[1 - c], qc, to_c)

    cuts = CORES if rows > 256 else 1

    def second(s, r):
        tt = turn(t, r, T)
        cols = pl.ds(pl.multiple_of(tt * feats + s * piece, piece), piece)
        size = rows // cuts
        for i in range(cuts):
            at = pl.ds(i * size, size)
            out = dot_nn(hid[at, :], wd[:, cols])
            back = dot_nt(gga[at, :], wg[cols, :]) + dot_nt(gup[at, :], wu[cols, :])
            shape = (CORES // cuts, B, A, group, piece)
            block = jnp.concatenate([out.reshape(shape), back.reshape(shape)], axis=3)
            block = block.astype(jnp.bfloat16)
            for j in range(CORES // cuts):
                parts[s, i + j, tt] = block[j]
        return send(parts.at[s, 1 - c, tt], landed.at[s, tt], to_c)

    def wide(value):
        return value.astype(jnp.float32)

    def narrow(value):
        return value.astype(jnp.bfloat16)

    def total(first_term, ref):
        value = wide(first_term)
        for i in range(ref.shape[0]):
            value = value + wide(ref[i])
        return value

    turns = list(range(1, T)) + [0]
    hops = [[] for _ in pieces]
    ends = [None] * PIECES
    cores = {}

    def hop(s, r):
        cores[s, r].wait_recv()
        tt = turn(t, r, T)
        sums[s, tt] = narrow(wide(parts[s, c, tt]) + wide(landed[s, tt]))
        for i, (rt, rb) in enumerate(offsets):
            if rt == r:
                source = sums.at[s, tt, turn(b, rb, B)]
                hops[s].append(send(source, rq.at[s, i], to_q[i]))

    def home(s):
        arrive(hops[s])
        v[s] = narrow(total(sums[s, t, b], rq.at[s]))
        ends[s] = [
            send(v.at[s, turn(a, r, A)], rz.at[s, r - 1], to_a[r - 1]) for r in range(1, A)
        ]

    before = None
    for s in pieces:
        for r in turns:
            cores[s, r] = second(s, r)
            if before is not None:
                hop(*before)
            else:
                ec.wait_recv()
                qc[...] = qr[c] + qc[...]
                qx[q] = qc[b]
                eq = [
                    send(qc.at[turn(b, j, B)], qx.at[q], peer)
                    for (i, j), peer in zip(offsets, to_q)
                ]
            before = (s, r)
    hop(*before)
    arrive(eq)
    qv[...] = total(qx[0], qx.at[pl.ds(1, T * B - 1)])
    kq = [send(qv.at[turn(a, r, A)], qz.at[r - 1], to_a[r - 1]) for r in range(1, A)]
    for s in pieces:
        home(s)
    for copy in started:
        copy.wait_send()
    arrive(kq)
    inner = total(qv[a], qz)
    place = lax.broadcasted_iota(jnp.int32, ids.shape, 1)
    result = jnp.zeros(ids.shape, jnp.float32)
    for k in range(ids.shape[1]):
        one = jnp.sum(jnp.where(lane == ids[:, k : k + 1], inner, 0.0), axis=1, keepdims=True)
        result = jnp.where(place == k, one, result)
    pgrad_ref[...] = result
    for s in pieces:
        arrive(ends[s])
        value = total(v[s, a], rz.at[s])
        at = pl.ds(s * piece, piece)
        mixed_ref[:, at] = narrow(value[:group])
        tgrad_ref[:, at] = narrow(value[group:])
    assert len(started) == count


def settle(*refs):
    for source, target in zip(refs[: len(refs) // 2], refs[len(refs) // 2 :]):
        target[...] = source[...]


def per_device(tokens, out_grad, expert_ids, gate_probs, w_gate, w_up, w_down):
    E = lax.axis_size("expert")
    T = lax.axis_size("tensor")
    A, B = grid_of(E)
    C, S = CORES, PIECES
    group, feats = tokens.shape
    width = feats * T
    hidden = w_gate.shape[2]
    rows = E * group
    lanes = -(-E // LANES) * LANES
    bf, f32 = jnp.bfloat16, jnp.float32
    pair = (2 * group, feats // PIECES)
    tile = (group, lanes)
    na, nb, nq = A - 1, B - 1, T * B - 1
    gather = S * (na + nq + 1) + na + nb + 1
    scatter = S * (T + nq + na) + 1 + nq + na
    count = gather + scatter

    def vm(*shape, dtype=bf):
        return pltpu.VMEM(shape, dtype)

    scratch = [
        vm(group, feats), vm(group, feats),
        vm(*expert_ids.shape, dtype=jnp.int32), vm(*gate_probs.shape, dtype=f32),
        vm(width, hidden), vm(width, hidden), vm(hidden, width),
        vm(S, C, T * B, A, *pair), vm(C, B, A, *tile, dtype=f32),
        vm(rows, width), vm(rows, width),
        vm(rows, hidden), vm(rows, hidden), vm(rows, hidden),
        vm(rows, hidden, dtype=f32), vm(rows, hidden, dtype=f32), vm(rows, hidden, dtype=f32),
        vm(S, C, T, B, A, *pair), vm(S, T, B, A, *pair), vm(S, T, B, A, *pair),
        vm(S, nq, A, *pair), vm(S, A, *pair), vm(S, na, *pair),
        vm(C, B, A, *tile, dtype=f32), vm(B, A, *tile, dtype=f32),
        vm(T * B, A, *tile, dtype=f32), vm(A, *tile, dtype=f32), vm(na, *tile, dtype=f32),
        pltpu.SemaphoreType.DMA((4,)),
        pltpu.SemaphoreType.DMA((3,)),
        pltpu.SemaphoreType.DMA((count,)),
        pltpu.SemaphoreType.DMA((count,)),
    ]
    inside = pl.BlockSpec(memory_space=pltpu.VMEM)
    outside = pl.BlockSpec(memory_space=pl.ANY)
    shapes = (
        jax.ShapeDtypeStruct((group, feats), bf),
        jax.ShapeDtypeStruct((group, feats), bf),
        jax.ShapeDtypeStruct(expert_ids.shape, f32),
    )
    results = pl.pallas_call(
        functools.partial(kernel, A, B, T, count),
        out_shape=shapes,
        in_specs=[outside] * 7,
        out_specs=(inside, inside, inside),
        scratch_shapes=scratch,
        compiler_params=pltpu.CompilerParams(
            collective_id=0, has_side_effects=True, vmem_limit_bytes=60 * 1024 * 1024
        ),
        cost_estimate=pl.CostEstimate(
            flops=12 * rows * width * hidden,
            bytes_accessed=6 * width * hidden,
            transcendentals=rows * hidden,
        ),
    )(tokens, out_grad, expert_ids, gate_probs, w_gate, w_up, w_down)
    return pl.pallas_call(
        settle, out_shape=shapes, in_specs=[inside] * 3, out_specs=(inside, inside, inside)
    )(*results)


def solution(mesh):
    placed = (
        P("expert", "tensor"),
        P("expert", "tensor"),
        P("expert", None),
        P("expert", None),
        P("expert", None, "tensor"),
        P("expert", None, "tensor"),
        P("expert", "tensor", None),
    )
    return jax.shard_map(
        per_device,
        mesh=mesh,
        in_specs=placed,
        out_specs=(P("expert", "tensor"), P("expert", "tensor"), P("expert", None)),
        check_vma=False,
    )
```
